256 devices in a mesh: tm: 32 (over z, x), sx: 2 (over core), sy: 4 (over y).
Axes of the slice: x: 4, y: 4, z: 8, core: 2. Of those that a mesh axis runs over, the one named last changes fastest.
Arguments:
- adjoint_guess: float32 [256, 2, 64, 2048], P('tm', None, 'sx', 'sy'), may hold values from -6 to 6
- sources: float32 [256, 2, 64, 2048], P('tm', None, 'sx', 'sy'), may hold values from -2 to 2
- velocities: bfloat16 [256, 2, 64, 2048], P('tm', None, 'sx', 'sy'), may hold values from -0.29882812 to 0.29882812
- c_points: int32 [32], replicated, may hold values from 0 to 7
Outputs:
- adjoint_iterate: float32 [256, 2, 64, 2048], P('tm', None, 'sx', 'sy')
The draws below stay inside these ranges and needn't reach their ends.
All inputs are finite; a program needn't handle non-finite values.
Results may differ from the reference program's by a relative error of at most 0.0003.
Values may be sent and summed in bfloat16 or wider, within the bound.
A program may use at most 64 MiB of HBM per device.

```python
import jax
import jax.numpy as jnp

TS = 8
NX = 64
NY = 2048
NT = 256
N_TM = 32


def draw_sources(key, part):
    key = jax.random.fold_in(key, 7)
    rough_key = jax.random.fold_in(key, 0)
    shape = (NT, 2, NX, NY)
    return jnp.clip(0.3 * jax.random.normal(rough_key, shape, jnp.float32), -1.8, 1.8)


def touch_ends(drawn, rng, low, largest):
    longest = drawn.shape.index(max(drawn.shape))
    spots = []
    for shift in (0, 1):
        where = [jax.random.randint(jax.random.fold_in(rng, axis), (), 0, length) for axis, length in enumerate(drawn.shape)]
        where[longest] = (where[longest] + shift) % drawn.shape[longest]
        spots.append(tuple(where))
    return drawn.at[spots[0]].set(low).at[spots[1]].set(largest)


def block_levels(own_key, extent, cuts, least, top_value):
    loudness, own = 1.0, jax.random.fold_in(own_key, 6)
    for position, parts in cuts:
        draws = jnp.exp(jax.random.uniform(jax.random.fold_in(own, position), (parts,), jnp.float32, least / len(cuts), top_value / len(cuts)))
        loudness = loudness * jnp.repeat(draws, extent[position] // parts).reshape([-1 if axis == position else 1 for axis in range(len(extent))])
    return loudness


def bell_draw(stream_key, extent, spread, bound, cuts=(), kind=jnp.bfloat16):
    entries = jax.random.normal(stream_key, extent, jnp.float32) * spread
    if len(cuts) > 0:
        entries = block_levels(stream_key, extent, cuts, -0.22, 0.18) * entries
    return jnp.clip(entries, min=-bound, max=bound).astype(kind)


def setup_inputs(seed: int = 0) -> dict:
    keys = jax.random.split(jax.random.key(seed), 5)
    return {
        "adjoint_guess": bell_draw(keys[0], (NT, 2, NX, NY), 1.0, 6.0, ((0, 32), (2, 2), (3, 4)), jnp.float32),
        "sources": draw_sources(jax.random.fold_in(keys[4], 71), 0),
        "velocities": jnp.clip(jax.random.uniform(keys[2], (NT, 2, NX, NY), jnp.float32, -0.29882812, 0.29882812) * block_levels(keys[2], (NT, 2, NX, NY), ((0, 32), (2, 2), (3, 4)), -0.4, 0.0), -0.29882812, 0.29882812).astype(jnp.bfloat16),
        "c_points": touch_ends(jax.random.randint(keys[3], (N_TM,), 0, TS), jax.random.fold_in(keys[3], 1), 0, TS - 1).astype(jnp.int32),
    }


VISCOSITY = 0.5
TIME_STEP = 1.0


def widen_zero(array, width):
    return jnp.pad(array, [(0, 0)] * (array.ndim - 2) + [(width, width), (width, width)])


def flow_terms(velocity):
    u_part = velocity[..., 0, :, :]
    w_part = velocity[..., 1, :, :]
    return (u_part[..., 1:-1, 1:-1], w_part[..., 1:-1, 1:-1],
            (u_part[..., 2:, 1:-1] - u_part[..., :-2, 1:-1]) * 0.5,
            (u_part[..., 1:-1, 2:] - u_part[..., 1:-1, :-2]) * 0.5,
            (w_part[..., 2:, 1:-1] - w_part[..., :-2, 1:-1]) * 0.5,
            (w_part[..., 1:-1, 2:] - w_part[..., 1:-1, :-2]) * 0.5)


def propagate(padded, terms, step_size):
    centre = padded[..., 1:-1, 1:-1]
    north = padded[..., 2:, 1:-1]
    south = padded[..., :-2, 1:-1]
    east = padded[..., 1:-1, 2:]
    west = padded[..., 1:-1, :-2]
    neighbours = north + south + east + west
    along_x = (north - south) * 0.5
    along_y = (east - west) * 0.5
    u_field, w_field, ux_field, uy_field, wx_field, wy_field = terms
    advect = u_field[..., None, :, :] * along_x + w_field[..., None, :, :] * along_y
    first = centre[..., 0, :, :]
    second = centre[..., 1, :, :]
    couple = jnp.stack([ux_field * first + wx_field * second, uy_field * first + wy_field * second], axis=-3)
    return (centre + step_size * (VISCOSITY * neighbours + advect - couple)) / (1.0 + 4.0 * VISCOSITY * step_size)


def reference(adjoint_guess, sources, velocities, c_points):
    groups = N_TM
    guess = adjoint_guess.reshape(groups, TS, 2, NX, NY)
    source = sources.reshape(groups, TS, 2, NX, NY)
    flow = velocities.reshape(groups, TS, 2, NX, NY)
    indices = jnp.arange(groups)
    slots = [guess[:, step] for step in range(TS)]
    field = guess[indices, c_points]
    for step in range(TS - 2, -1, -1):
        terms = flow_terms(widen_zero(flow[:, step].astype(jnp.float32), 1))
        update = propagate(widen_zero(field, 1), terms, TIME_STEP) + source[:, step]
        active = (step < c_points)[:, None, None, None]
        field = jnp.where(active, update, field)
        slots[step] = jnp.where(active, update, slots[step])
    field = jnp.concatenate([field[1:], jnp.zeros_like(field[:1])], axis=0)
    residual = jnp.zeros_like(field)
    for step in range(TS - 1, -1, -1):
        terms = flow_terms(widen_zero(flow[:, step].astype(jnp.float32), 1))
        update = propagate(widen_zero(field, 1), terms, TIME_STEP) + source[:, step]
        above = (step > c_points)[:, None, None, None]
        here = (step == c_points)[:, None, None, None]
        slots[step] = jnp.where(above, update, slots[step])
        residual = jnp.where(here, update - guess[:, step], residual)
        field = jnp.where(above, update, field)
    c_after = jnp.concatenate([c_points[1:], jnp.zeros((1,), jnp.int32)])
    spans = (TS + c_after - c_points).astype(jnp.float32)
    coarse_terms = flow_terms(widen_zero(flow[indices, c_points].astype(jnp.float32), 1))
    error = jnp.zeros((2, NX, NY), jnp.float32)
    corrections = []
    for group in range(groups - 1, -1, -1):
        terms = tuple(part[group] for part in coarse_terms)
        error = propagate(widen_zero(error, 1), terms, TIME_STEP * spans[group]) + residual[group]
        corrections.append(error)
    corrections = jnp.stack(corrections[::-1], axis=0)
    relaxed = jnp.stack(slots, axis=1)
    result = relaxed.at[indices, c_points].set(guess[indices, c_points] + corrections)
    return result.reshape(NT, 2, NX, NY)
```

```python
import jax
import jax.numpy as jnp
from jax import lax
from jax.experimental import pallas as pl
from jax.experimental.pallas import tpu as pltpu
from jax.sharding import PartitionSpec as P

F32 = jnp.float32
MESH = pl.DeviceIdType.MESH
STEPS = 8
ROWS = 32
COLS = 512
EDGE = 8
XROWS = ROWS + EDGE
XCOLS = COLS + 128
GROUPS = 32
TILES = 16
REACH = 16
LEVELS = 16


def iota(shape, dim):
    return lax.broadcasted_iota(jnp.int32, shape, dim)


def roll(x, shift, dim):
    return pltpu.roll(x, shift % x.shape[dim], dim)


def pack_edges(tiles, first):
    lane = iota((ROWS, 128), 1)
    packed = jnp.zeros((ROWS, 128), F32)
    for place, tile in enumerate(tiles):
        at = EDGE * place
        moved = roll(tile(), at if first else at + EDGE, 1)
        packed = jnp.where((lane >= at) & (lane < at + EDGE), moved, packed)
    return packed


def unpack_edges(right, left, place):
    lane = iota((XROWS, 128), 1)
    at = EDGE * place
    return jnp.where(lane < 64, roll(right, -at, 1), roll(left, -EDGE - at, 1))


def window(read, index):
    lane = iota((ROWS, 128), 1)
    tile, offset = divmod(32 * index - REACH, 128)

    def part(component, target):
        piece = read(component, tile % 4)
        if offset + 64 > 128:
            piece = jnp.where(lane >= offset, piece, read(component, (tile + 1) % 4))
        return roll(piece, target - offset, 1)

    return jnp.where(lane < 64, part(0, 0), part(1, 64))


def owner_of(tile):
    z = tile // 2
    return z * 4 + 2 * (tile % 2) + z % 2


def kernel(
    c_ref, guess, src, vel, out,
    srcx, velx, fld, nxt, co1, pk, pkr, fp, fpr, res, rw, vw,
    rbuf, xbuf, vbuf, vxbuf, coef, ebuf, ebox, nbr,
    s_a, r_a, s_b, r_b, s_v, r_v, s_r, r_r, r_rx, s_e, r_e, s_n, r_n,
):
    tm = lax.axis_index("tm")
    sx = lax.axis_index("sx")
    sy = lax.axis_index("sy")
    east = lax.rem(sy + 1, 4)
    west = lax.rem(sy + 3, 4)
    before = lax.rem(tm + GROUPS - 1, GROUPS)
    edge_row = pl.multiple_of((1 - sx) * (ROWS - EDGE), 8)
    edge = pl.ds(edge_row, EDGE)
    halo = pl.ds(ROWS, EDGE)
    here = c_ref[tm]
    z = tm // 4
    x = lax.rem(tm, 4)
    tile = 2 * z + x // 2
    is_owner = (sx == 0) & (lax.rem(x, 2) == lax.rem(z, 2))
    is_end = is_owner & ((tile == 0) | (tile == TILES - 1))

    def remote(src_ref, dst_ref, send, recv, device):
        return pltpu.make_async_remote_copy(
            src_ref=src_ref, dst_ref=dst_ref, send_sem=send, recv_sem=recv,
            device_id=device, device_id_type=MESH,
        )

    def arrived(ref, sem):
        pltpu.make_async_copy(ref, ref, sem).wait()

    srcx[:, :, 0:ROWS, 0:COLS] = src[...]
    velx[:, :, 0:ROWS, 0:COLS] = vel[...].astype(F32)
    fld[0, :, 0:ROWS, 0:COLS] = guess[here]
    own = pl.ds(0, COLS)
    copies = [
        remote(src.at[:, :, edge, :], srcx.at[:, :, halo, own], s_a.at[0], r_a.at[0], (tm, 1 - sx, sy)),
        remote(velx.at[:, :, edge, own], velx.at[:, :, halo, own], s_a.at[1], r_a.at[1], (tm, 1 - sx, sy)),
        remote(fld.at[0, :, edge, own], fld.at[0, :, halo, own], s_a.at[2], r_a.at[2], (tm, 1 - sx, sy)),
    ]
    for copy in copies:
        copy.start()
    for way, (first, lanes, target) in enumerate(
        ((True, slice(0, 128), west), (False, slice(COLS - 128, COLS), east))
    ):
        pairs = [(j, k) for j in range(STEPS) for k in range(2)]
        pk[way, 0] = pack_edges([lambda j=j, k=k: src[j, k, :, lanes] for j, k in pairs], first)
        pk[way, 1] = pack_edges([lambda j=j, k=k: velx[j, k, 0:ROWS, lanes] for j, k in pairs], first)
        pk[way, 2] = pack_edges([lambda k=k: fld[0, k, 0:ROWS, lanes] for k in range(2)], first)
        for copy in (
            remote(pk.at[way], pkr.at[way, :, 0:ROWS], s_a.at[3 + way], r_a.at[3 + way], (tm, sx, target)),
            remote(
                pk.at[way, :, edge], pkr.at[way, :, halo], s_a.at[5 + way], r_a.at[5 + way], (tm, 1 - sx, target)
            ),
        ):
            copy.start()
            copies.append(copy)

    def read_velocity(component, lane_tile):
        return vel[here, component, :, 128 * lane_tile : 128 * lane_tile + 128].astype(F32)

    for index in range(-1, TILES + 1):
        vw[index + 1] = window(read_velocity, index).astype(jnp.bfloat16)

    half = pl.ds(pl.multiple_of(sx * ROWS, ROWS), ROWS)

    def is_self(index):
        return (owner_of(index) == tm) & (sx == 0)

    def to_windows(source, boxes, extras, send, recv, recv_extra, act):
        def one(index, _):
            mine = is_self(index)

            @pl.when(mine)
            def _():
                if act:
                    pltpu.make_async_copy(source.at[index + 1], boxes.at[tm, half], send.at[index + 1]).start()

            @pl.when(jnp.logical_not(mine))
            def _():
                copy = remote(
                    source.at[index + 1], boxes.at[tm, half], send.at[index + 1], recv(tm), (owner_of(index), 0, sy)
                )
                copy.start() if act else copy.wait_send()

            return 0

        lax.fori_loop(0, TILES, one, 0)
        for index, target, device in ((0, west, owner_of(TILES - 1)), (TILES + 1, east, owner_of(0))):
            copy = remote(source.at[index], extras.at[tm, half], send.at[index], recv_extra(tm), (device, 0, target))
            copy.start() if act else copy.wait_send()

    def own_window(source, boxes, send):
        @pl.when(is_owner)
        def _():
            pltpu.make_async_copy(source.at[tile + 1], boxes.at[tm, half], send.at[tile + 1]).wait()

    to_windows(vw, vbuf, vxbuf, s_v, lambda g: r_v.at[g, 0], lambda g: r_v.at[g, 1], True)

    for copy in copies:
        copy.wait()
    to_right = jnp.where(sy < 3, 1.0, 0.0).astype(F32)
    to_left = jnp.where(sy > 0, 1.0, 0.0).astype(F32)
    right = [pkr[0, part] * to_right for part in range(3)]
    left = [pkr[1, part] * to_left for part in range(3)]
    for j in range(STEPS):
        for k in range(2):
            srcx[j, k, :, COLS:XCOLS] = unpack_edges(right[0], left[0], 2 * j + k)
            velx[j, k, :, COLS:XCOLS] = unpack_edges(right[1], left[1], 2 * j + k)
    for k in range(2):
        fld[0, k, :, COLS:XCOLS] = unpack_edges(right[2], left[2], k)

    lane = iota((EDGE, XCOLS), 1)
    row = iota((EDGE, XCOLS), 0)
    inside = (lane < COLS) | ((lane < COLS + 64) & (sy < 3)) | ((lane >= COLS + 64) & (sy > 0))
    third = jnp.where(inside, 1.0 / 3.0, 0.0).astype(F32)
    tiles = XROWS // EDGE
    last_own = ROWS // EDGE - 1
    north_ok = jnp.where((row == EDGE - 1) & (sx == 1), 0.0, 1.0).astype(F32)
    south_ok = jnp.where((row == 0) & (sx == 0), 0.0, 1.0).astype(F32)

    def around(parts):
        up = [roll(part, -1, 0) for part in parts]
        down = [roll(part, 1, 0) for part in parts]
        for i, part in enumerate(parts):
            north = jnp.where(row == EDGE - 1, up[(i + 1) % tiles], up[i])
            south = jnp.where(row == 0, down[i - 1], down[i])
            yield part, north, south, roll(part, -1, 1), roll(part, 1, 1)

    def coefficients(j, _):
        u = [velx[j, 0, EDGE * i : EDGE * (i + 1), :] for i in range(tiles)]
        w = [velx[j, 1, EDGE * i : EDGE * (i + 1), :] for i in range(tiles)]
        for i, ((uc, un, us, ue, uw), (wc, wn, ws, we, ww)) in enumerate(zip(around(u), around(w))):
            rows = slice(EDGE * i, EDGE * (i + 1))
            scale_n = scale_s = third
            if i == last_own:
                un, wn, scale_n = un * north_ok, wn * north_ok, third * north_ok
            if i == 0:
                us, ws, scale_s = us * south_ok, ws * south_ok, third * south_ok
            hu, hw = 0.5 * uc, 0.5 * wc
            ht = 0.5 * third
            co1[j, 0, rows] = third - ht * (un - us)
            co1[j, 1, rows] = -ht * (wn - ws)
            co1[j, 2, rows] = third - ht * (we - ww)
            co1[j, 3, rows] = -ht * (ue - uw)
            co1[j, 4, rows] = scale_n * (0.5 + hu)
            co1[j, 5, rows] = scale_s * (0.5 - hu)
            co1[j, 6, rows] = third * (0.5 + hw)
            co1[j, 7, rows] = third * (0.5 - hw)
        return 0

    lax.fori_loop(0, STEPS, coefficients, 0)

    def phi(field, slot, j):
        p = [field[slot, 0, EDGE * i : EDGE * (i + 1), :] for i in range(tiles)]
        q = [field[slot, 1, EDGE * i : EDGE * (i + 1), :] for i in range(tiles)]
        for i, ((pc, pn, ps, pe, pw), (qc, qn, qs, qe, qw)) in enumerate(zip(around(p), around(q))):
            rows = slice(EDGE * i, EDGE * (i + 1))
            a = [co1[j, n, rows] for n in range(8)]
            new_p = a[0] * pc + a[1] * qc + a[4] * pn + a[5] * ps + a[6] * pe + a[7] * pw + srcx[j, 0, rows]
            new_q = a[2] * qc + a[3] * pc + a[4] * qn + a[5] * qs + a[6] * qe + a[7] * qw + srcx[j, 1, rows]
            yield rows, i, ((0, pc, new_p), (1, qc, new_q))

    def lower(turn, _):
        j = STEPS - 2 - turn
        slot = lax.rem(turn, 2)
        active = j < here
        for rows, i, parts in phi(fld, slot, j):
            for k, old, new in parts:
                fld[1 - slot, k, rows] = jnp.where(active, new, old)
                if i <= last_own:
                    out[j, k, rows] = new[:, 0:COLS]
        return 0

    lax.fori_loop(0, STEPS - 1, lower, 0)
    out[STEPS - 1] = guess[STEPS - 1]
    done = (STEPS - 1) % 2

    relays = [
        remote(fld.at[done, :, 0:ROWS, own], nxt.at[0, :, 0:ROWS, own], s_b.at[0], r_b.at[0], (before, sx, sy)),
        remote(fld.at[done, :, edge, own], nxt.at[0, :, halo, own], s_b.at[1], r_b.at[1], (before, 1 - sx, sy)),
    ]
    for copy in relays:
        copy.start()
    for way, (first, lanes, target) in enumerate(
        ((True, slice(0, 128), west), (False, slice(COLS - 128, COLS), east))
    ):
        fp[way] = pack_edges([lambda k=k: fld[done, k, 0:ROWS, lanes] for k in range(2)], first)
        for copy in (
            remote(fp.at[way], fpr.at[way, 0:ROWS], s_b.at[2 + way], r_b.at[2 + way], (before, sx, target)),
            remote(fp.at[way, edge], fpr.at[way, halo], s_b.at[4 + way], r_b.at[4 + way], (before, 1 - sx, target)),
        ):
            copy.start()
            relays.append(copy)
    for copy in relays:
        copy.wait_recv()
    for k in range(2):
        nxt[0, k, :, COLS:XCOLS] = unpack_edges(fpr[0] * to_right, fpr[1] * to_left, k)

    @pl.when(tm == GROUPS - 1)
    def _():
        nxt[0] = jnp.zeros((2, XROWS, XCOLS), F32)

    def upper(turn, _):
        j = STEPS - 1 - turn
        slot = lax.rem(turn, 2)
        above = j > here
        coarse = j == here
        for rows, i, parts in phi(nxt, slot, j):
            for k, old, new in parts:
                nxt[1 - slot, k, rows] = jnp.where(above, new, old)
                if i <= last_own:
                    inner = new[:, 0:COLS]
                    out[j, k, rows] = jnp.where(above, inner, out[j, k, rows])
                    res[k, rows] = jnp.where(coarse, inner - guess[j, k, rows], res[k, rows])
        return 0

    res[...] = jnp.zeros((2, ROWS, COLS), F32)
    lax.fori_loop(0, STEPS, upper, 0)

    def read_residual(component, lane_tile):
        return res[component, :, 128 * lane_tile : 128 * lane_tile + 128]

    for index in range(-1, TILES + 1):
        rw[index + 1] = window(read_residual, index)
    to_windows(rw, rbuf, xbuf, s_r, lambda g: r_r.at[g], lambda g: r_rx.at[g], True)

    @pl.when(is_owner)
    def _():
        lane = iota((2 * ROWS, 128), 1)
        grid_row = iota((2 * ROWS, 128), 0)
        place = lax.rem(lane, 64)
        first = lane < 64
        from_extra = ((place < REACH) & (tile == 0)) | ((place >= 64 - REACH) & (tile == TILES - 1))
        outside = ((place < REACH) & (tile == 0) & (sy == 0)) | (
            (place >= 64 - REACH) & (tile == TILES - 1) & (sy == 3)
        )
        keep = jnp.where(outside, 0.0, 1.0).astype(F32)
        north = jnp.where(grid_row == 2 * ROWS - 1, 0.0, 1.0).astype(F32)
        south = jnp.where(grid_row == 0, 0.0, 1.0).astype(F32)
        own_window(vw, vbuf, s_v)
        own_window(rw, rbuf, s_r)

        def wait_velocity(level, _):
            pl.when(level != tm)(lambda: arrived(vbuf.at[level], r_v.at[level, 0]))
            pl.when(level == tm)(lambda: arrived(vbuf.at[level, ROWS : 2 * ROWS], r_v.at[level, 0]))
            return 0

        lax.fori_loop(0, GROUPS, wait_velocity, 0)

        @pl.when(is_end)
        def _():
            def merge(level, _):
                arrived(vxbuf.at[level], r_v.at[level, 1])
                both = jnp.where(from_extra, vxbuf[level].astype(F32), vbuf[level].astype(F32))
                vbuf[level] = both.astype(jnp.bfloat16)
                return 0

            lax.fori_loop(0, GROUPS, merge, 0)

        def coarse_coefficients(level, _):
            v = vbuf[level].astype(F32) * keep
            after = jnp.where(level + 1 < GROUPS, c_ref[jnp.minimum(level + 1, GROUPS - 1)], 0)
            span = jnp.full((2 * ROWS, 128), STEPS + after - c_ref[level], jnp.int32).astype(F32)
            inverse = keep / (1.0 + 2.0 * span)
            k = span * inverse
            swapped = roll(v, 64, 1)
            u = jnp.where(first, v, swapped)
            w = jnp.where(first, swapped, v)
            dx = 0.5 * (roll(v, -1, 0) * north - roll(v, 1, 0) * south)
            dy = 0.5 * (roll(v, -1, 1) - roll(v, 1, 1))
            coef[level, 0] = inverse - k * jnp.where(first, dx, dy)
            coef[level, 1] = -k * jnp.where(first, roll(dx, 64, 1), roll(dy, 64, 1))
            coef[level, 2] = k * (0.5 + 0.5 * u) * north
            coef[level, 3] = k * (0.5 - 0.5 * u) * south
            coef[level, 4] = k * (0.5 + 0.5 * w)
            coef[level, 5] = k * (0.5 - 0.5 * w)
            return 0

        lax.fori_loop(0, GROUPS, coarse_coefficients, 0)

        def send_error(level, act):
            for core in range(2):
                rows = pl.ds(core * ROWS, ROWS)

                def away(core=core, rows=rows):
                    copy = remote(
                        ebuf.at[level, rows], ebox.at[tile], s_e.at[level, core], r_e.at[tile], (level, core, sy)
                    )
                    copy.start() if act else copy.wait_send()

                if core == 1:
                    away()
                else:
                    pl.when(level != tm)(away)

                    @pl.when(level == tm)
                    def _():
                        if act:
                            pltpu.make_async_copy(ebuf.at[level, rows], ebox.at[tile], r_e.at[tile]).start()

        def solve(top):
            def one(turn, error):
                level = top - turn
                pl.when(level != tm)(lambda: arrived(rbuf.at[level], r_r.at[level]))
                pl.when(level == tm)(lambda: arrived(rbuf.at[level, ROWS : 2 * ROWS], r_r.at[level]))

                @pl.when(is_end)
                def _():
                    arrived(xbuf.at[level], r_rx.at[level])
                    rbuf[level] = jnp.where(from_extra, xbuf[level], rbuf[level])

                c = [coef[level, n] for n in range(6)]
                new = c[0] * error + c[1] * roll(error, 64, 1)
                new = new + (c[2] * roll(error, -1, 0) + c[3] * roll(error, 1, 0))
                new = new + (c[4] * roll(error, -1, 1) + c[5] * roll(error, 1, 1))
                new = new + rbuf[level] * keep
                ebuf[level] = new
                send_error(level, True)
                return new

            return one

        error = lax.fori_loop(0, LEVELS, solve(GROUPS - 1), jnp.zeros((2 * ROWS, 128), F32))
        middle = GROUPS - LEVELS
        right_tile = lax.rem(tile + 1, TILES)
        left_tile = lax.rem(tile + TILES - 1, TILES)
        right_sy = jnp.where(tile == TILES - 1, east, sy)
        left_sy = jnp.where(tile == 0, west, sy)
        sides = [
            remote(ebuf.at[middle], nbr.at[0], s_n.at[0], r_n.at[0], (owner_of(right_tile), 0, right_sy)),
            remote(ebuf.at[middle], nbr.at[1], s_n.at[1], r_n.at[1], (owner_of(left_tile), 0, left_sy)),
        ]
        for copy in sides:
            copy.start()
        for copy in sides:
            copy.wait_recv()
        error = jnp.where(place < REACH, roll(nbr[0], -32, 1), error)
        error = jnp.where(place >= 64 - REACH, roll(nbr[1], 32, 1), error) * keep
        lax.fori_loop(0, LEVELS, solve(middle - 1), error)
        for copy in sides:
            copy.wait_send()

        def wait_errors(level, _):
            send_error(level, False)
            return 0

        lax.fori_loop(0, GROUPS, wait_errors, 0)

    def wait_boxes(index, _):
        arrived(ebox.at[index], r_e.at[index])
        return 0

    lax.fori_loop(0, TILES, wait_boxes, 0)
    lane = iota((ROWS, 128), 1)
    for k in range(2):
        for lane_tile in range(4):
            whole = None
            for i in range(4):
                piece = roll(ebox[4 * lane_tile + i], 32 * i - REACH - 64 * k, 1)
                whole = piece if whole is None else jnp.where(lane >= 32 * i, piece, whole)
            res[k, :, 128 * lane_tile : 128 * lane_tile + 128] = whole

    def place_coarse(j, _):
        out[j] = jnp.where(j == here, guess[j] + res[...], out[j])
        return 0

    lax.fori_loop(0, STEPS, place_coarse, 0)

    for copy in relays:
        copy.wait_send()
    to_windows(vw, vbuf, vxbuf, s_v, lambda g: r_v.at[g, 0], lambda g: r_v.at[g, 1], False)
    to_windows(rw, rbuf, xbuf, s_r, lambda g: r_r.at[g], lambda g: r_rx.at[g], False)


def shards(adjoint_guess, sources, velocities, c_points):
    dma = pltpu.SemaphoreType.DMA
    vmem = pl.BlockSpec(memory_space=pltpu.VMEM)
    return pl.pallas_call(
        kernel,
        out_shape=jax.ShapeDtypeStruct(adjoint_guess.shape, F32),
        in_specs=[pl.BlockSpec(memory_space=pltpu.SMEM), vmem, vmem, vmem],
        out_specs=vmem,
        scratch_shapes=[
            pltpu.VMEM((STEPS, 2, XROWS, XCOLS), F32),
            pltpu.VMEM((STEPS, 2, XROWS, XCOLS), F32),
            pltpu.VMEM((2, 2, XROWS, XCOLS), F32),
            pltpu.VMEM((2, 2, XROWS, XCOLS), F32),
            pltpu.VMEM((STEPS, 8, XROWS, XCOLS), F32),
            pltpu.VMEM((2, 3, ROWS, 128), F32),
            pltpu.VMEM((2, 3, XROWS, 128), F32),
            pltpu.VMEM((2, ROWS, 128), F32),
            pltpu.VMEM((2, XROWS, 128), F32),
            pltpu.VMEM((2, ROWS, COLS), F32),
            pltpu.VMEM((TILES + 2, ROWS, 128), F32),
            pltpu.VMEM((TILES + 2, ROWS, 128), jnp.bfloat16),
            pltpu.VMEM((GROUPS, 2 * ROWS, 128), F32),
            pltpu.VMEM((GROUPS, 2 * ROWS, 128), F32),
            pltpu.VMEM((GROUPS, 2 * ROWS, 128), jnp.bfloat16),
            pltpu.VMEM((GROUPS, 2 * ROWS, 128), jnp.bfloat16),
            pltpu.VMEM((GROUPS, 6, 2 * ROWS, 128), F32),
            pltpu.VMEM((GROUPS, 2 * ROWS, 128), F32),
            pltpu.VMEM((TILES, ROWS, 128), F32),
            pltpu.VMEM((2, 2 * ROWS, 128), F32),
            dma((7,)), dma((7,)), dma((6,)), dma((6,)),
            dma((TILES + 2,)), dma((GROUPS, 2)),
            dma((TILES + 2,)), dma((GROUPS,)), dma((GROUPS,)),
            dma((GROUPS, 2)), dma((TILES,)), dma((2,)), dma((2,)),
        ],
        compiler_params=pltpu.CompilerParams(has_side_effects=True, vmem_limit_bytes=48 * 1024 * 1024),
    )(c_points, adjoint_guess, sources, velocities)


def solution(mesh):
    placed = (P("tm", None, "sx", "sy"), P("tm", None, "sx", "sy"), P("tm", None, "sx", "sy"), P())
    return jax.shard_map(
        shards, mesh=mesh, in_specs=placed, out_specs=P("tm", None, "sx", "sy"), check_vma=False
    )
```

```python
import jax
import jax.numpy as jnp
from jax import lax
from jax.experimental import pallas as pl
from jax.experimental.pallas import tpu as pltpu
from jax.sharding import PartitionSpec as P

F32 = jnp.float32
MESH = pl.DeviceIdType.MESH
STEPS = 8
ROWS = 32
COLS = 512
EDGE = 8
XROWS = ROWS + EDGE
XCOLS = COLS + 128
GROUPS = 32
TILES = 16
REACH = 16
BATCH = 4
LEVELS = 16


def iota(shape, dim):
    return lax.broadcasted_iota(jnp.int32, shape, dim)


def roll(x, shift, dim):
    return pltpu.roll(x, shift % x.shape[dim], dim)


def pack_edges(tiles, first):
    lane = iota((ROWS, 128), 1)
    packed = jnp.zeros((ROWS, 128), F32)
    for place, tile in enumerate(tiles):
        at = EDGE * place
        moved = roll(tile(), at if first else at + EDGE, 1)
        packed = jnp.where((lane >= at) & (lane < at + EDGE), moved, packed)
    return packed


def unpack_edges(right, left, place):
    lane = iota((XROWS, 128), 1)
    at = EDGE * place
    return jnp.where(lane < 64, roll(right, -at, 1), roll(left, -EDGE - at, 1))


def window(read, index):
    lane = iota((ROWS, 128), 1)
    tile, offset = divmod(32 * index - REACH, 128)

    def part(component, target):
        piece = read(component, tile % 4)
        if offset + 64 > 128:
            piece = jnp.where(lane >= offset, piece, read(component, (tile + 1) % 4))
        return roll(piece, target - offset, 1)

    return jnp.where(lane < 64, part(0, 0), part(1, 64))


def fold(part, step):
    lane = lax.rem(iota((EDGE, 128), 1), 64)
    at = 0 if step > 0 else 48
    folded = part[0:EDGE]
    for i in range(1, ROWS // EDGE):
        moved = roll(part[EDGE * i : EDGE * (i + 1)], step * i, 1)
        folded = jnp.where((lane >= at + step * i) & (lane < at + step * i + REACH), moved, folded)
    return folded


def owner_of(tile):
    z = tile // 2
    return z * 4 + 2 * (tile % 2) + z % 2


def kernel(
    c_hbm, guess_hbm, src_hbm, vel_hbm, out,
    c_ref, guess, vel, srcx, velx, fld, nxt, co1, pk, pkr, fp, fpr, res, upd, rw, rf, vw, vf,
    rbuf, xbuf, vbuf, vxbuf, coef, ebuf, ebox, mine, nbr,
    s_a, r_a, s_b, r_b, s_v, r_v, s_r, r_r, r_rx, s_e, r_e, s_n, r_n, s_i, known,
):
    tm = lax.axis_index("tm")
    sx = lax.axis_index("sx")
    sy = lax.axis_index("sy")
    east = lax.rem(sy + 1, 4)
    west = lax.rem(sy + 3, 4)
    before = lax.rem(tm + GROUPS - 1, GROUPS)
    edge_row = pl.multiple_of((1 - sx) * (ROWS - EDGE), 8)
    edge = pl.ds(edge_row, EDGE)
    halo = pl.ds(ROWS, EDGE)
    z = tm // 4
    x = lax.rem(tm, 4)
    tile = 2 * z + x // 2
    is_owner = (sx == 0) & (lax.rem(x, 2) == lax.rem(z, 2))
    is_end = is_owner & ((tile == 0) | (tile == TILES - 1))

    def remote(src_ref, dst_ref, send, recv, device):
        return pltpu.make_async_remote_copy(
            src_ref=src_ref, dst_ref=dst_ref, send_sem=send, recv_sem=recv,
            device_id=device, device_id_type=MESH,
        )

    def arrived(ref, sem):
        pltpu.make_async_copy(ref, ref, sem).wait()

    barrier = pltpu.get_barrier_semaphore()

    def greet(*device):
        pl.semaphore_signal(barrier, inc=1, device_id=device, device_id_type=MESH)

    fetch = [
        pltpu.make_async_copy(c_hbm, c_ref, s_i.at[0]),
        pltpu.make_async_copy(vel_hbm, vel, s_i.at[1]),
        pltpu.make_async_copy(src_hbm, srcx.at[:, :, 0:ROWS, 0:COLS], s_i.at[2]),
        pltpu.make_async_copy(guess_hbm, guess, s_i.at[3]),
    ]
    for copy in fetch:
        copy.start()
    column_groups = [lax.rem(tm + 4 * step, GROUPS) for step in range(1, 8)]
    for group in column_groups:
        greet(group, sx, sy)
    for step in range(4):
        group = 4 * z + lax.rem(x + step, 4)
        for core in (sx, 1 - sx):
            for column in (sy, west, east):
                if step > 0 or core is not sx or column is not sy:
                    greet(group, core, column)

    for copy in fetch:
        copy.wait()
    here = c_ref[tm]

    velx[:, :, 0:ROWS, 0:COLS] = vel[...].astype(F32)
    fld[0, :, 0:ROWS, 0:COLS] = guess[here]
    own = pl.ds(0, COLS)
    copies = [
        remote(srcx.at[:, :, edge, own], srcx.at[:, :, halo, own], s_a.at[0], r_a.at[0], (tm, 1 - sx, sy)),
        remote(velx.at[:, :, edge, own], velx.at[:, :, halo, own], s_a.at[1], r_a.at[1], (tm, 1 - sx, sy)),
        remote(fld.at[0, :, edge, own], fld.at[0, :, halo, own], s_a.at[2], r_a.at[2], (tm, 1 - sx, sy)),
    ]
    sides = ((True, slice(0, 128), west), (False, slice(COLS - 128, COLS), east))
    for way, (first_columns, lanes, target) in enumerate(sides):
        pairs = [(j, k) for j in range(STEPS) for k in range(2)]
        pk[way, 0] = pack_edges([lambda j=j, k=k: srcx[j, k, 0:ROWS, lanes] for j, k in pairs], first_columns)
        pk[way, 1] = pack_edges([lambda j=j, k=k: velx[j, k, 0:ROWS, lanes] for j, k in pairs], first_columns)
        pk[way, 2] = pack_edges([lambda k=k: fld[0, k, 0:ROWS, lanes] for k in range(2)], first_columns)
        copies.append(
            remote(pk.at[way], pkr.at[way, :, 0:ROWS], s_a.at[3 + way], r_a.at[3 + way], (tm, sx, target))
        )
        copies.append(
            remote(
                pk.at[way, :, edge], pkr.at[way, :, halo], s_a.at[5 + way], r_a.at[5 + way], (tm, 1 - sx, target)
            )
        )
    pl.semaphore_wait(barrier, 4 * 2 * 3 - 1 + 7)
    for copy in reversed(copies):
        copy.start()

    for group in column_groups:
        pl.semaphore_signal(known, inc=1, device_id=(group, sx, sy), device_id_type=MESH)

    def read_velocity(component, lane_tile):
        return vel[here, component, :, 128 * lane_tile : 128 * lane_tile + 128].astype(F32)

    half = pl.ds(pl.multiple_of(sx * ROWS, ROWS), ROWS)

    def is_self(index):
        return (owner_of(index) == tm) & (sx == 0)

    eighth = pl.ds(pl.multiple_of(sx * EDGE, EDGE), EDGE)

    def pack_ends(read, folded):
        folded[0] = fold(window(read, -1), -REACH)
        folded[1] = fold(window(read, TILES), REACH)

    def pack_window(read, source, index):
        source[index] = window(read, index).astype(source.dtype)

    def ends(folded, extras, send, recv):
        for side, target, device in ((0, west, owner_of(TILES - 1)), (1, east, owner_of(0))):
            yield remote(folded.at[side], extras.at[tm, eighth], send.at[TILES + side], recv(tm), (device, 0, target))

    def to_windows(source, boxes, send, recv, act):
        def one(turn, _):
            index = lax.rem(tile + turn, TILES)
            mine = is_self(index)

            @pl.when(mine)
            def _():
                if act:
                    pltpu.make_async_copy(source.at[index], boxes.at[tm, half], recv(tm)).start()

            @pl.when(jnp.logical_not(mine))
            def _():
                copy = remote(source.at[index], boxes.at[tm, half], send.at[index], recv(tm), (owner_of(index), 0, sy))
                copy.start() if act else copy.wait_send()

            return 0

        lax.fori_loop(0, TILES, one, 0)

    pack_ends(read_velocity, vf)
    for index in range(TILES):
        pack_window(read_velocity, vw, index)
    out[STEPS - 1] = guess[STEPS - 1]

    pl.semaphore_wait(known, 7)
    for copy in ends(vf, vxbuf, s_v, lambda g: r_v.at[g, 1]):
        copy.start()
    to_windows(vw, vbuf, s_v, lambda g: r_v.at[g, 0], True)
    for copy in copies:
        copy.wait()
    to_right = jnp.where(sy < 3, 1.0, 0.0).astype(F32)
    to_left = jnp.where(sy > 0, 1.0, 0.0).astype(F32)
    right = [pkr[0, part] * to_right for part in range(3)]
    left = [pkr[1, part] * to_left for part in range(3)]
    for j in range(STEPS):
        for k in range(2):
            srcx[j, k, :, COLS:XCOLS] = unpack_edges(right[0], left[0], 2 * j + k)
            velx[j, k, :, COLS:XCOLS] = unpack_edges(right[1], left[1], 2 * j + k)
    for k in range(2):
        fld[0, k, :, COLS:XCOLS] = unpack_edges(right[2], left[2], k)

    lane = iota((EDGE, XCOLS), 1)
    row = iota((EDGE, XCOLS), 0)
    inside = (lane < COLS) | ((lane < COLS + 64) & (sy < 3)) | ((lane >= COLS + 64) & (sy > 0))
    third = jnp.where(inside, 1.0 / 3.0, 0.0).astype(F32)
    tiles = XROWS // EDGE
    last_own = ROWS // EDGE - 1
    north_ok = jnp.where((row == EDGE - 1) & (sx == 1), 0.0, 1.0).astype(F32)
    south_ok = jnp.where((row == 0) & (sx == 0), 0.0, 1.0).astype(F32)

    def around(parts):
        up = [roll(part, -1, 0) for part in parts]
        down = [roll(part, 1, 0) for part in parts]
        for i, part in enumerate(parts):
            north = jnp.where(row == EDGE - 1, up[(i + 1) % tiles], up[i])
            south = jnp.where(row == 0, down[i - 1], down[i])
            yield part, north, south, roll(part, -1, 1), roll(part, 1, 1)

    def coefficients(j, _):
        u = [velx[j, 0, EDGE * i : EDGE * (i + 1), :] for i in range(tiles)]
        w = [velx[j, 1, EDGE * i : EDGE * (i + 1), :] for i in range(tiles)]
        for i, ((uc, un, us, ue, uw), (wc, wn, ws, we, ww)) in enumerate(zip(around(u), around(w))):
            rows = slice(EDGE * i, EDGE * (i + 1))
            scale_n = scale_s = third
            if i == last_own:
                un, wn, scale_n = un * north_ok, wn * north_ok, third * north_ok
            if i == 0:
                us, ws, scale_s = us * south_ok, ws * south_ok, third * south_ok
            hu, hw = 0.5 * uc, 0.5 * wc
            ht = 0.5 * third
            co1[j, 0, rows] = third - ht * (un - us)
            co1[j, 1, rows] = -ht * (wn - ws)
            co1[j, 2, rows] = third - ht * (we - ww)
            co1[j, 3, rows] = -ht * (ue - uw)
            co1[j, 4, rows] = scale_n * (0.5 + hu)
            co1[j, 5, rows] = scale_s * (0.5 - hu)
            co1[j, 6, rows] = third * (0.5 + hw)
            co1[j, 7, rows] = third * (0.5 - hw)
        return 0

    lax.fori_loop(0, STEPS - 1, coefficients, 0)

    def phi(field, slot, j):
        p = [field[slot, 0, EDGE * i : EDGE * (i + 1), :] for i in range(tiles)]
        q = [field[slot, 1, EDGE * i : EDGE * (i + 1), :] for i in range(tiles)]
        for i, ((pc, pn, ps, pe, pw), (qc, qn, qs, qe, qw)) in enumerate(zip(around(p), around(q))):
            rows = slice(EDGE * i, EDGE * (i + 1))
            a = [co1[j, n, rows] for n in range(8)]
            new_p = a[0] * pc + a[1] * qc + a[4] * pn + a[5] * ps + a[6] * pe + a[7] * pw + srcx[j, 0, rows]
            new_q = a[2] * qc + a[3] * pc + a[4] * qn + a[5] * qs + a[6] * qe + a[7] * qw + srcx[j, 1, rows]
            yield rows, i, ((0, pc, new_p), (1, qc, new_q))

    def lower(turn, _):
        j = STEPS - 2 - turn
        slot = lax.rem(turn, 2)
        active = j < here
        for rows, i, parts in phi(fld, slot, j):
            for k, old, new in parts:
                fld[1 - slot, k, rows] = jnp.where(active, new, old)
                if i <= last_own:
                    out[j, k, rows] = new[:, 0:COLS]
        return 0

    lax.fori_loop(0, STEPS - 1, lower, 0)
    done = (STEPS - 1) % 2

    relays = [
        remote(fld.at[done, :, 0:ROWS, own], nxt.at[0, :, 0:ROWS, own], s_b.at[0], r_b.at[0], (before, sx, sy)),
        remote(fld.at[done, :, edge, own], nxt.at[0, :, halo, own], s_b.at[1], r_b.at[1], (before, 1 - sx, sy)),
    ]
    for copy in relays:
        copy.start()
    for way, (first, lanes, target) in enumerate(
        ((True, slice(0, 128), west), (False, slice(COLS - 128, COLS), east))
    ):
        fp[way] = pack_edges([lambda k=k: fld[done, k, 0:ROWS, lanes] for k in range(2)], first)
        for copy in (
            remote(fp.at[way], fpr.at[way, 0:ROWS], s_b.at[2 + way], r_b.at[2 + way], (before, sx, target)),
            remote(fp.at[way, edge], fpr.at[way, halo], s_b.at[4 + way], r_b.at[4 + way], (before, 1 - sx, target)),
        ):
            copy.start()
            relays.append(copy)
    coefficients(STEPS - 1, 0)

    for copy in relays:
        copy.wait_recv()
    for k in range(2):
        nxt[0, k, :, COLS:XCOLS] = unpack_edges(fpr[0] * to_right, fpr[1] * to_left, k)

    @pl.when(tm == GROUPS - 1)
    def _():
        nxt[0] = jnp.zeros((2, XROWS, XCOLS), F32)

    def upper(turn, _):
        j = STEPS - 1 - turn
        slot = lax.rem(turn, 2)
        above = j > here
        coarse = j == here
        for rows, i, parts in phi(nxt, slot, j):
            for k, old, new in parts:
                nxt[1 - slot, k, rows] = jnp.where(above, new, old)
                if i <= last_own:
                    inner = new[:, 0:COLS]
                    out[j, k, rows] = jnp.where(above, inner, out[j, k, rows])
                    upd[k, rows] = jnp.where(coarse, inner, upd[k, rows])
        return 0

    upd[...] = jnp.zeros((2, ROWS, COLS), F32)
    lax.fori_loop(0, STEPS, upper, 0)

    res[...] = upd[...] - guess[here]

    def read_residual(component, lane_tile):
        return res[component, :, 128 * lane_tile : 128 * lane_tile + 128]

    pack_ends(read_residual, rf)
    for copy in ends(rf, xbuf, s_r, lambda g: r_rx.at[g]):
        copy.start()
    for index in range(TILES):
        pack_window(read_residual, rw, index)
    to_windows(rw, rbuf, s_r, lambda g: r_r.at[g], True)

    window_lane = iota((2 * ROWS, 128), 1)
    grid_row = iota((2 * ROWS, 128), 0)
    place = lax.rem(window_lane, 64)
    first = window_lane < 64
    from_extra = ((place < REACH) & (tile == 0)) | ((place >= 64 - REACH) & (tile == TILES - 1))
    outside = ((place < REACH) & (tile == 0) & (sy == 0)) | (
        (place >= 64 - REACH) & (tile == TILES - 1) & (sy == 3)
    )
    valid = (place[0 : ROWS // 2] >= REACH) & (place[0 : ROWS // 2] < 64 - REACH)
    keep = jnp.where(outside, 0.0, 1.0).astype(F32)
    top_open = jnp.where(grid_row == 2 * ROWS - 1, 0.0, 1.0).astype(F32)
    bottom_open = jnp.where(grid_row == 0, 0.0, 1.0).astype(F32)

    def unfold(part):
        pieces = [part[EDGE * core : EDGE * (core + 1)] for core in range(2)]
        step = jnp.where(tile == 0, 128 - REACH, REACH)
        return jnp.concatenate(
            [pltpu.roll(piece, lax.rem(step * i, 128), 1) for piece in pieces for i in range(ROWS // EDGE)], 0
        )

    @pl.when(is_owner)
    def _():
        def wait_velocity(level, _):
            arrived(vbuf.at[level], r_v.at[level, 0])
            return 0

        def merge(level, _):
            arrived(vxbuf.at[level], r_v.at[level, 1])
            both = jnp.where(from_extra, unfold(vxbuf[level]), vbuf[level].astype(F32))
            vbuf[level] = both.astype(jnp.bfloat16)
            return 0

        def coarse_coefficients(level, _):
            v = vbuf[level].astype(F32) * keep
            after = jnp.where(level + 1 < GROUPS, c_ref[jnp.minimum(level + 1, GROUPS - 1)], 0)
            span = jnp.full((1, 128), STEPS + after - c_ref[level], jnp.int32).astype(F32)
            inverse = keep * (1.0 / (1.0 + 2.0 * span))
            k = span * inverse
            swapped = roll(v, 64, 1)
            u = jnp.where(first, v, swapped)
            w = jnp.where(first, swapped, v)
            dx = 0.5 * (roll(v, -1, 0) * top_open - roll(v, 1, 0) * bottom_open)
            dy = 0.5 * (roll(v, -1, 1) - roll(v, 1, 1))
            coef[level, 0] = inverse - k * jnp.where(first, dx, dy)
            coef[level, 1] = -k * jnp.where(first, roll(dx, 64, 1), roll(dy, 64, 1))
            coef[level, 2] = k * (0.5 + 0.5 * u) * top_open
            coef[level, 3] = k * (0.5 - 0.5 * u) * bottom_open
            coef[level, 4] = k * (0.5 + 0.5 * w)
            coef[level, 5] = k * (0.5 - 0.5 * w)
            return 0

        def prepare(low, high):
            lax.fori_loop(low, high, wait_velocity, 0)

            @pl.when(is_end)
            def _():
                lax.fori_loop(low, high, merge, 0)

            lax.fori_loop(low, high, coarse_coefficients, 0)

        prepare(GROUPS - LEVELS, GROUPS)

        def send_error(level, core):
            own = (level == tm) & (core == 0)
            slot = jnp.where(own, TILES, tile)
            to_core = jnp.where(own, 1, core)
            return remote(
                ebuf.at[level, core], ebox.at[slot], s_e.at[level, core], r_e.at[slot], (level, to_core, sy)
            )

        def solve(top):
            def several(turn, error):
                first_level = top - BATCH * turn
                for n in range(BATCH):
                    arrived(rbuf.at[first_level - n], r_r.at[first_level - n])

                @pl.when(is_end)
                def _():
                    for n in range(BATCH):
                        level = first_level - n
                        arrived(xbuf.at[level], r_rx.at[level])
                        rbuf[level] = jnp.where(from_extra, unfold(xbuf[level]), rbuf[level])

                for n in range(BATCH):
                    level = first_level - n
                    c = [coef[level, n] for n in range(6)]
                    new = c[0] * error + c[1] * roll(error, 64, 1)
                    new = new + (c[2] * roll(error, -1, 0) + c[3] * roll(error, 1, 0))
                    new = new + (c[4] * roll(error, -1, 1) + c[5] * roll(error, 1, 1))
                    error = new + rbuf[level] * keep
                    for core in range(2):
                        low = new[ROWS * core : ROWS * core + ROWS // 2]
                        high = new[ROWS * core + ROWS // 2 : ROWS * (core + 1)]
                        piece = jnp.where(valid, low, roll(high, 32, 1))
                        ebuf[level, core] = piece
                        if core == 0:
                            ebox[tile] = jnp.where(level == tm, piece, ebox[tile])
                        send_error(level, core).start()
                return error

            return several

        error = lax.fori_loop(0, LEVELS // BATCH, solve(GROUPS - 1), jnp.zeros((2 * ROWS, 128), F32))
        mine[...] = error
        right_tile = lax.rem(tile + 1, TILES)
        left_tile = lax.rem(tile + TILES - 1, TILES)
        right_sy = jnp.where(tile == TILES - 1, east, sy)
        left_sy = jnp.where(tile == 0, west, sy)
        sides = [
            remote(mine, nbr.at[0], s_n.at[0], r_n.at[0], (owner_of(right_tile), 0, right_sy)),
            remote(mine, nbr.at[1], s_n.at[1], r_n.at[1], (owner_of(left_tile), 0, left_sy)),
        ]
        for copy in sides:
            copy.start()
        prepare(0, GROUPS - LEVELS)
        for copy in sides:
            copy.wait_recv()
        error = jnp.where(place < REACH, roll(nbr[0], -32, 1), error)
        error = jnp.where(place >= 64 - REACH, roll(nbr[1], 32, 1), error) * keep
        lax.fori_loop(0, LEVELS // BATCH, solve(GROUPS - LEVELS - 1), error)
        for copy in sides:
            copy.wait_send()

        def wait_errors(level, _):
            for core in range(2):
                send_error(level, core).wait_send()
            return 0

        lax.fori_loop(0, GROUPS, wait_errors, 0)

    def wait_boxes(index, _):
        pl.when(jnp.logical_not(is_owner & (index == tile)))(lambda: arrived(ebox.at[index], r_e.at[index]))
        return 0

    lax.fori_loop(0, TILES, wait_boxes, 0)

    @pl.when((sx == 1) & (lax.rem(x, 2) == lax.rem(z, 2)))
    def _():
        arrived(ebox.at[TILES], r_e.at[TILES])

    lane = iota((ROWS // 2, 128), 1)
    for part in range(2):
        rows = slice(part * ROWS // 2, (part + 1) * ROWS // 2)
        for k in range(2):
            for lane_tile in range(4):
                whole = None
                for i in range(4):
                    piece = roll(ebox[4 * lane_tile + i], 32 * i - REACH - 64 * k - 32 * part, 1)
                    whole = piece if whole is None else jnp.where(lane >= 32 * i, piece, whole)
                lanes = slice(128 * lane_tile, 128 * lane_tile + 128)
                upd[k, rows, lanes] = upd[k, rows, lanes] + whole

    def place_coarse(j, _):
        out[j] = jnp.where(j == here, upd[...], out[j])
        return 0

    lax.fori_loop(0, STEPS, place_coarse, 0)

    for copy in relays:
        copy.wait_send()
    for copy in (*ends(vf, vxbuf, s_v, lambda g: r_v.at[g, 1]), *ends(rf, xbuf, s_r, lambda g: r_rx.at[g])):
        copy.wait_send()
    to_windows(vw, vbuf, s_v, lambda g: r_v.at[g, 0], False)
    to_windows(rw, rbuf, s_r, lambda g: r_r.at[g], False)


def shards(adjoint_guess, sources, velocities, c_points):
    dma = pltpu.SemaphoreType.DMA
    vmem = pl.BlockSpec(memory_space=pltpu.VMEM)
    return pl.pallas_call(
        kernel,
        out_shape=jax.ShapeDtypeStruct(adjoint_guess.shape, F32),
        in_specs=[pl.BlockSpec(memory_space=pltpu.HBM)] * 4,
        out_specs=vmem,
        scratch_shapes=[
            pltpu.SMEM((GROUPS,), jnp.int32),
            pltpu.VMEM((STEPS, 2, ROWS, COLS), F32),
            pltpu.VMEM((STEPS, 2, ROWS, COLS), jnp.bfloat16),
            pltpu.VMEM((STEPS, 2, XROWS, XCOLS), F32),
            pltpu.VMEM((STEPS, 2, XROWS, XCOLS), F32),
            pltpu.VMEM((2, 2, XROWS, XCOLS), F32),
            pltpu.VMEM((2, 2, XROWS, XCOLS), F32),
            pltpu.VMEM((STEPS, 8, XROWS, XCOLS), F32),
            pltpu.VMEM((2, 3, ROWS, 128), F32),
            pltpu.VMEM((2, 3, XROWS, 128), F32),
            pltpu.VMEM((2, ROWS, 128), F32),
            pltpu.VMEM((2, XROWS, 128), F32),
            pltpu.VMEM((2, ROWS, COLS), F32),
            pltpu.VMEM((2, ROWS, COLS), F32),
            pltpu.VMEM((TILES, ROWS, 128), F32),
            pltpu.VMEM((2, EDGE, 128), F32),
            pltpu.VMEM((TILES, ROWS, 128), jnp.bfloat16),
            pltpu.VMEM((2, EDGE, 128), F32),
            pltpu.VMEM((GROUPS, 2 * ROWS, 128), F32),
            pltpu.VMEM((GROUPS, 2 * EDGE, 128), F32),
            pltpu.VMEM((GROUPS, 2 * ROWS, 128), jnp.bfloat16),
            pltpu.VMEM((GROUPS, 2 * EDGE, 128), F32),
            pltpu.VMEM((GROUPS, 6, 2 * ROWS, 128), F32),
            pltpu.VMEM((GROUPS, 2, ROWS // 2, 128), F32),
            pltpu.VMEM((TILES + 1, ROWS // 2, 128), F32),
            pltpu.VMEM((2 * ROWS, 128), F32),
            pltpu.VMEM((2, 2 * ROWS, 128), F32),
            dma((7,)), dma((7,)), dma((6,)), dma((6,)),
            dma((TILES + 2,)), dma((GROUPS, 2)),
            dma((TILES + 2,)), dma((GROUPS,)), dma((GROUPS,)),
            dma((GROUPS, 2)), dma((TILES + 1,)), dma((2,)), dma((2,)), dma((4,)), pltpu.SemaphoreType.REGULAR,
        ],
        compiler_params=pltpu.CompilerParams(has_side_effects=True, collective_id=0, vmem_limit_bytes=60 * 1024 * 1024),
    )(c_points, adjoint_guess, sources, velocities)


def solution(mesh):
    placed = (P("tm", None, "sx", "sy"), P("tm", None, "sx", "sy"), P("tm", None, "sx", "sy"), P())
    return jax.shard_map(
        shards, mesh=mesh, in_specs=placed, out_specs=P("tm", None, "sx", "sy"), check_vma=False
    )
```

```python
import jax
import jax.numpy as jnp
from jax import lax
from jax.experimental import pallas as pl
from jax.experimental.pallas import tpu as pltpu
from jax.sharding import PartitionSpec as P

F32 = jnp.float32
MESH = pl.DeviceIdType.MESH
STEPS = 8
ROWS = 32
COLS = 512
EDGE = 8
XROWS = ROWS + EDGE
XCOLS = COLS + 128
GROUPS = 32
TILES = 16
WHOLE = 32000.0
REACH = 16
BATCH = 4
LEVELS = 16


def iota(shape, dim):
    return lax.broadcasted_iota(jnp.int32, shape, dim)


def roll(x, shift, dim):
    return pltpu.roll(x, shift % x.shape[dim], dim)


def pack_edges(tiles, first):
    lane = iota((ROWS, 128), 1)
    packed = jnp.zeros((ROWS, 128), F32)
    for place, tile in enumerate(tiles):
        at = EDGE * place
        moved = roll(tile(), at if first else at + EDGE, 1)
        packed = jnp.where((lane >= at) & (lane < at + EDGE), moved, packed)
    return packed


def unpack_edges(right, left, place):
    lane = iota((XROWS, 128), 1)
    at = EDGE * place
    return jnp.where(lane < 64, roll(right, -at, 1), roll(left, -EDGE - at, 1))


def window(read, index):
    lane = iota((ROWS, 128), 1)
    tile, offset = divmod(32 * index - REACH, 128)

    def part(component, target):
        piece = read(component, tile % 4)
        if offset + 64 > 128:
            piece = jnp.where(lane >= offset, piece, read(component, (tile + 1) % 4))
        return roll(piece, target - offset, 1)

    return jnp.where(lane < 64, part(0, 0), part(1, 64))


def fold(part, step):
    lane = lax.rem(iota((EDGE, 128), 1), 64)
    at = 0 if step > 0 else 48
    folded = part[0:EDGE]
    for i in range(1, ROWS // EDGE):
        moved = roll(part[EDGE * i : EDGE * (i + 1)], step * i, 1)
        folded = jnp.where((lane >= at + step * i) & (lane < at + step * i + REACH), moved, folded)
    return folded


def owner_of(tile):
    z = tile // 2
    return z * 4 + 2 * (tile % 2) + z % 2


def kernel(
    c_hbm, guess_hbm, src_hbm, vel_hbm, out,
    c_ref, guess, vel, srcx, velx, fld, nxt, co1, pk, pkr, fp, fpr, fq, nq, fs, ns, ff, nf, res, upd, rw, rf, vw, vf,
    rbuf, xbuf, vbuf, vxbuf, coef, dec, ebuf, ebox, mine, nbr,
    s_a, r_a, s_b, r_b, s_v, r_v, r_vx, s_r, r_r, r_rx, s_e, r_e, s_n, r_n, s_i, known,
):
    tm = lax.axis_index("tm")
    sx = lax.axis_index("sx")
    sy = lax.axis_index("sy")
    east = lax.rem(sy + 1, 4)
    west = lax.rem(sy + 3, 4)
    before = lax.rem(tm + GROUPS - 1, GROUPS)
    edge_row = pl.multiple_of((1 - sx) * (ROWS - EDGE), 8)
    edge = pl.ds(edge_row, EDGE)
    halo = pl.ds(ROWS, EDGE)
    z = tm // 4
    x = lax.rem(tm, 4)
    tile = 2 * z + x // 2
    is_owner = (sx == 0) & (lax.rem(x, 2) == lax.rem(z, 2))
    is_end = is_owner & ((tile == 0) | (tile == TILES - 1))

    def remote(src_ref, dst_ref, send, recv, device):
        return pltpu.make_async_remote_copy(
            src_ref=src_ref, dst_ref=dst_ref, send_sem=send, recv_sem=recv,
            device_id=device, device_id_type=MESH,
        )

    def arrived(ref, sem):
        pltpu.make_async_copy(ref, ref, sem).wait()

    barrier = pltpu.get_barrier_semaphore()

    def greet(*device):
        pl.semaphore_signal(barrier, inc=1, device_id=device, device_id_type=MESH)

    fetch = [
        pltpu.make_async_copy(c_hbm, c_ref, s_i.at[0]),
        pltpu.make_async_copy(vel_hbm, vel, s_i.at[1]),
        pltpu.make_async_copy(src_hbm, srcx.at[:, :, 0:ROWS, 0:COLS], s_i.at[2]),
        pltpu.make_async_copy(guess_hbm, guess, s_i.at[3]),
    ]
    for copy in fetch:
        copy.start()
    column_groups = [lax.rem(tm + 4 * step, GROUPS) for step in range(1, 8)]
    for group in column_groups:
        greet(group, sx, sy)
    for step in range(4):
        group = 4 * z + lax.rem(x + step, 4)
        for core in (sx, 1 - sx):
            for column in (sy, west, east):
                if step > 0 or core is not sx or column is not sy:
                    greet(group, core, column)

    for copy in fetch:
        copy.wait()
    here = c_ref[tm]

    velx[:, :, 0:ROWS, 0:COLS] = vel[...].astype(F32)
    fld[0, :, 0:ROWS, 0:COLS] = guess[here]
    own = pl.ds(0, COLS)
    copies = [
        remote(srcx.at[:, :, edge, own], srcx.at[:, :, halo, own], s_a.at[0], r_a.at[0], (tm, 1 - sx, sy)),
        remote(velx.at[:, :, edge, own], velx.at[:, :, halo, own], s_a.at[1], r_a.at[1], (tm, 1 - sx, sy)),
        remote(fld.at[0, :, edge, own], fld.at[0, :, halo, own], s_a.at[2], r_a.at[2], (tm, 1 - sx, sy)),
    ]
    sides = ((True, slice(0, 128), west), (False, slice(COLS - 128, COLS), east))
    for way, (first_columns, lanes, target) in enumerate(sides):
        pairs = [(j, k) for j in range(STEPS) for k in range(2)]
        pk[way, 0] = pack_edges([lambda j=j, k=k: srcx[j, k, 0:ROWS, lanes] for j, k in pairs], first_columns)
        pk[way, 1] = pack_edges([lambda j=j, k=k: velx[j, k, 0:ROWS, lanes] for j, k in pairs], first_columns)
        pk[way, 2] = pack_edges([lambda k=k: fld[0, k, 0:ROWS, lanes] for k in range(2)], first_columns)
        copies.append(
            remote(pk.at[way], pkr.at[way, :, 0:ROWS], s_a.at[3 + way], r_a.at[3 + way], (tm, sx, target))
        )
        copies.append(
            remote(
                pk.at[way, :, edge], pkr.at[way, :, halo], s_a.at[5 + way], r_a.at[5 + way], (tm, 1 - sx, target)
            )
        )
    pl.semaphore_wait(barrier, 4 * 2 * 3 - 1 + 7)
    for copy in reversed(copies):
        copy.start()

    for group in column_groups:
        pl.semaphore_signal(known, inc=1, device_id=(group, sx, sy), device_id_type=MESH)

    def read_velocity(component, lane_tile):
        return vel[here, component, :, 128 * lane_tile : 128 * lane_tile + 128].astype(F32)

    half = pl.ds(pl.multiple_of(sx * ROWS, ROWS), ROWS)

    def is_self(index):
        return (owner_of(index) == tm) & (sx == 0)

    eighth = pl.ds(pl.multiple_of(sx * EDGE, EDGE), EDGE)

    def pack_ends(read, folded):
        folded[0] = fold(window(read, -1), -REACH)
        folded[1] = fold(window(read, TILES), REACH)

    def ends(folded, extras, send, recv):
        for side, target, device in ((0, west, owner_of(TILES - 1)), (1, east, owner_of(0))):
            yield remote(folded.at[side], extras.at[tm, eighth], send.at[TILES + side], recv(tm), (device, 0, target))

    def to_windows(source, boxes, send, recv, act):
        def one(turn, _):
            index = lax.rem(tile + turn, TILES)
            mine = is_self(index)

            @pl.when(mine)
            def _():
                if act:
                    pltpu.make_async_copy(source.at[index], boxes.at[tm, half], recv(tm)).start()

            @pl.when(jnp.logical_not(mine))
            def _():
                copy = remote(source.at[index], boxes.at[tm, half], send.at[index], recv(tm), (owner_of(index), 0, sy))
                copy.start() if act else copy.wait_send()

            return 0

        lax.fori_loop(0, TILES, one, 0)

    pack_ends(read_velocity, vf)
    for index in range(TILES):
        vw[index] = window(read_velocity, index).astype(jnp.bfloat16)
    out[STEPS - 1] = guess[STEPS - 1]

    pl.semaphore_wait(known, 7)
    for copy in ends(vf, vxbuf, s_v, lambda g: r_vx.at[g]):
        copy.start()
    to_windows(vw, vbuf, s_v, lambda g: r_v.at[g // LEVELS], True)
    for copy in copies:
        copy.wait()
    to_right = jnp.where(sy < 3, 1.0, 0.0).astype(F32)
    to_left = jnp.where(sy > 0, 1.0, 0.0).astype(F32)
    right = [pkr[0, part] * to_right for part in range(3)]
    left = [pkr[1, part] * to_left for part in range(3)]
    for j in range(STEPS):
        for k in range(2):
            srcx[j, k, :, COLS:XCOLS] = unpack_edges(right[0], left[0], 2 * j + k)
            velx[j, k, :, COLS:XCOLS] = unpack_edges(right[1], left[1], 2 * j + k)
    for k in range(2):
        fld[0, k, :, COLS:XCOLS] = unpack_edges(right[2], left[2], k)

    lane = iota((EDGE, XCOLS), 1)
    row = iota((EDGE, XCOLS), 0)
    inside = (lane < COLS) | ((lane < COLS + 64) & (sy < 3)) | ((lane >= COLS + 64) & (sy > 0))
    third = jnp.where(inside, 1.0 / 3.0, 0.0).astype(F32)
    tiles = XROWS // EDGE
    last_own = ROWS // EDGE - 1
    north_ok = jnp.where((row == EDGE - 1) & (sx == 1), 0.0, 1.0).astype(F32)
    south_ok = jnp.where((row == 0) & (sx == 0), 0.0, 1.0).astype(F32)

    def around(parts):
        up = [roll(part, -1, 0) for part in parts]
        down = [roll(part, 1, 0) for part in parts]
        for i, part in enumerate(parts):
            north = jnp.where(row == EDGE - 1, up[(i + 1) % tiles], up[i])
            south = jnp.where(row == 0, down[i - 1], down[i])
            yield part, north, south, roll(part, -1, 1), roll(part, 1, 1)

    def coefficients(j, _):
        u = [velx[j, 0, EDGE * i : EDGE * (i + 1), :] for i in range(tiles)]
        w = [velx[j, 1, EDGE * i : EDGE * (i + 1), :] for i in range(tiles)]
        for i, ((uc, un, us, ue, uw), (wc, wn, ws, we, ww)) in enumerate(zip(around(u), around(w))):
            rows = slice(EDGE * i, EDGE * (i + 1))
            scale_n = scale_s = third
            if i == last_own:
                un, wn, scale_n = un * north_ok, wn * north_ok, third * north_ok
            if i == 0:
                us, ws, scale_s = us * south_ok, ws * south_ok, third * south_ok
            hu, hw = 0.5 * uc, 0.5 * wc
            ht = 0.5 * third
            co1[j, 0, rows] = third - ht * (un - us)
            co1[j, 1, rows] = -ht * (wn - ws)
            co1[j, 2, rows] = third - ht * (we - ww)
            co1[j, 3, rows] = -ht * (ue - uw)
            co1[j, 4, rows] = scale_n * (0.5 + hu)
            co1[j, 5, rows] = scale_s * (0.5 - hu)
            co1[j, 6, rows] = third * (0.5 + hw)
            co1[j, 7, rows] = third * (0.5 - hw)
        return 0

    lax.fori_loop(0, STEPS - 1, coefficients, 0)

    def phi(field, slot, j):
        p = [field[slot, 0, EDGE * i : EDGE * (i + 1), :] for i in range(tiles)]
        q = [field[slot, 1, EDGE * i : EDGE * (i + 1), :] for i in range(tiles)]
        for i, ((pc, pn, ps, pe, pw), (qc, qn, qs, qe, qw)) in enumerate(zip(around(p), around(q))):
            rows = slice(EDGE * i, EDGE * (i + 1))
            a = [co1[j, n, rows] for n in range(8)]
            new_p = a[0] * pc + a[1] * qc + a[4] * pn + a[5] * ps + a[6] * pe + a[7] * pw + srcx[j, 0, rows]
            new_q = a[2] * qc + a[3] * pc + a[4] * qn + a[5] * qs + a[6] * qe + a[7] * qw + srcx[j, 1, rows]
            yield rows, i, ((0, pc, new_p), (1, qc, new_q))

    def lower(turn, _):
        j = STEPS - 2 - turn
        slot = lax.rem(turn, 2)
        active = j < here
        for rows, i, parts in phi(fld, slot, j):
            for k, old, new in parts:
                fld[1 - slot, k, rows] = jnp.where(active, new, old)
                if i <= last_own:
                    out[j, k, rows] = new[:, 0:COLS]
        return 0

    lax.fori_loop(0, STEPS - 1, lower, 0)
    done = (STEPS - 1) % 2

    largest = jnp.max(jnp.abs(fld[done, :, 0:ROWS, 0:COLS]), axis=(0, 2))[:, None]
    power = jnp.floor(8.0 * jnp.log2(jnp.maximum(largest, 1e-30))) + 2.0
    to_unit = WHOLE * jnp.exp2(-0.125 * power)
    for k in range(2):
        fq[k] = jnp.floor(fld[done, k, 0:ROWS, 0:COLS] * to_unit + 0.5).astype(jnp.int32).astype(jnp.int16)
    quarter = iota((EDGE, 128), 1) // 32
    spread = jnp.broadcast_to(power, (ROWS, 128))
    scales = spread[0:EDGE]
    for i in range(1, ROWS // EDGE):
        scales = jnp.where(quarter == i, spread[EDGE * i : EDGE * (i + 1)], scales)
    fs[...] = scales
    relays = [
        remote(fld.at[done, :, edge, own], nxt.at[0, :, halo, own], s_b.at[1], r_b.at[1], (before, 1 - sx, sy)),
        remote(fq, nq, s_b.at[0], r_b.at[0], (before, sx, sy)),
        remote(fs, ns, s_b.at[6], r_b.at[6], (before, sx, sy)),
    ]
    for way, (first_columns, lanes, target) in enumerate(sides):
        fp[way] = pack_edges([lambda k=k: fld[done, k, 0:ROWS, lanes] for k in range(2)], first_columns)
        sixteenth = iota((EDGE, 128), 1) // (2 * EDGE)
        folded = fp[way, 0:EDGE]
        for i in range(1, ROWS // EDGE):
            moved = roll(fp[way, EDGE * i : EDGE * (i + 1)], 2 * EDGE * i, 1)
            folded = jnp.where(sixteenth == i, moved, folded)
        ff[way] = folded
        relays.append(remote(ff.at[way], nf.at[way], s_b.at[2 + way], r_b.at[2 + way], (before, sx, target)))
        relays.append(
            remote(fp.at[way, edge], fpr.at[way], s_b.at[4 + way], r_b.at[4 + way], (before, 1 - sx, target))
        )
    for copy in reversed(relays):
        copy.start()
    coefficients(STEPS - 1, 0)

    for copy in relays:
        copy.wait_recv()
    got = [
        jnp.concatenate([roll(nf[way], -2 * EDGE * i, 1) for i in range(ROWS // EDGE)] + [fpr[way]], 0)
        for way in range(2)
    ]
    for k in range(2):
        nxt[0, k, :, COLS:XCOLS] = unpack_edges(got[0] * to_right, got[1] * to_left, k)
    scales = ns[...]
    unit = jnp.concatenate(
        [jnp.broadcast_to(scales[:, 32 * i : 32 * i + 1], (EDGE, 128)) for i in range(ROWS // EDGE)], 0
    )
    unit = jnp.exp2(0.125 * unit) * (1.0 / WHOLE)
    for k in range(2):
        for lane_tile in range(COLS // 128):
            lanes = slice(128 * lane_tile, 128 * lane_tile + 128)
            nxt[0, k, 0:ROWS, lanes] = nq[k, :, lanes].astype(jnp.int32).astype(F32) * unit

    @pl.when(tm == GROUPS - 1)
    def _():
        nxt[0] = jnp.zeros((2, XROWS, XCOLS), F32)

    def upper(turn, _):
        j = STEPS - 1 - turn
        slot = lax.rem(turn, 2)
        above = j > here
        coarse = j == here
        for rows, i, parts in phi(nxt, slot, j):
            for k, old, new in parts:
                nxt[1 - slot, k, rows] = jnp.where(above, new, old)
                if i <= last_own:
                    inner = new[:, 0:COLS]
                    out[j, k, rows] = jnp.where(above, inner, out[j, k, rows])
                    upd[k, rows] = jnp.where(coarse, inner, upd[k, rows])
        return 0

    upd[...] = jnp.zeros((2, ROWS, COLS), F32)
    lax.fori_loop(0, STEPS, upper, 0)

    res[...] = upd[...] - guess[here]

    def read_residual(component, lane_tile):
        return res[component, :, 128 * lane_tile : 128 * lane_tile + 128]

    pack_ends(read_residual, rf)
    for copy in ends(rf, xbuf, s_r, lambda g: r_rx.at[g]):
        copy.start()
    largest = jnp.max(jnp.abs(res[...]), axis=(0, 2))[:, None]
    power = jnp.floor(8.0 * jnp.log2(jnp.maximum(largest, 1e-30))) + 2.0
    power = jnp.broadcast_to(power, (ROWS, 128))
    to_unit = WHOLE * jnp.exp2(-0.125 * power)
    first_lane = iota((ROWS, 128), 1) == 0
    for index in range(TILES):
        piece = jnp.floor(window(read_residual, index) * to_unit + 0.5)
        rw[index] = jnp.where(first_lane, power, piece).astype(jnp.int32).astype(jnp.int16)
    to_windows(rw, rbuf, s_r, lambda g: r_r.at[g // BATCH], True)

    window_lane = iota((2 * ROWS, 128), 1)
    grid_row = iota((2 * ROWS, 128), 0)
    place = lax.rem(window_lane, 64)
    first = window_lane < 64
    from_extra = ((place < REACH) & (tile == 0)) | ((place >= 64 - REACH) & (tile == TILES - 1))
    outside = ((place < REACH) & (tile == 0) & (sy == 0)) | (
        (place >= 64 - REACH) & (tile == TILES - 1) & (sy == 3)
    )
    valid = (place[0 : ROWS // 2] >= REACH) & (place[0 : ROWS // 2] < 64 - REACH)
    keep = jnp.where(outside, 0.0, 1.0).astype(F32)
    top_open = jnp.where(grid_row == 2 * ROWS - 1, 0.0, 1.0).astype(F32)
    bottom_open = jnp.where(grid_row == 0, 0.0, 1.0).astype(F32)

    def unfold(part):
        pieces = [part[EDGE * core : EDGE * (core + 1)] for core in range(2)]
        step = jnp.where(tile == 0, 128 - REACH, REACH)
        return jnp.concatenate(
            [pltpu.roll(piece, lax.rem(step * i, 128), 1) for piece in pieces for i in range(ROWS // EDGE)], 0
        )

    @pl.when(is_owner)
    def _():
        def merge(level, _):
            arrived(vxbuf.at[level], r_vx.at[level])
            both = jnp.where(from_extra, unfold(vxbuf[level]), vbuf[level].astype(F32))
            vbuf[level] = both.astype(jnp.bfloat16)
            return 0

        def coarse_coefficients(level, _):
            v = vbuf[level].astype(F32) * keep
            after = jnp.where(level + 1 < GROUPS, c_ref[jnp.minimum(level + 1, GROUPS - 1)], 0)
            span = jnp.full((1, 128), STEPS + after - c_ref[level], jnp.int32).astype(F32)
            inverse = keep * (1.0 / (1.0 + 2.0 * span))
            k = span * inverse
            swapped = roll(v, 64, 1)
            u = jnp.where(first, v, swapped)
            w = jnp.where(first, swapped, v)
            dx = 0.5 * (roll(v, -1, 0) * top_open - roll(v, 1, 0) * bottom_open)
            dy = 0.5 * (roll(v, -1, 1) - roll(v, 1, 1))
            coef[level, 0] = inverse - k * jnp.where(first, dx, dy)
            coef[level, 1] = -k * jnp.where(first, roll(dx, 64, 1), roll(dy, 64, 1))
            coef[level, 2] = k * (0.5 + 0.5 * u) * top_open
            coef[level, 3] = k * (0.5 - 0.5 * u) * bottom_open
            coef[level, 4] = k * (0.5 + 0.5 * w)
            coef[level, 5] = k * (0.5 - 0.5 * w)
            return 0

        def prepare(low, high):
            arrived(vbuf.at[low:high], r_v.at[low // LEVELS])

            @pl.when(is_end)
            def _():
                lax.fori_loop(low, high, merge, 0)

            lax.fori_loop(low, high, coarse_coefficients, 0)

        prepare(GROUPS - LEVELS, GROUPS)

        def send_error(level, core):
            own = (level == tm) & (core == 0)
            slot = jnp.where(own, TILES, tile)
            to_core = jnp.where(own, 1, core)
            return remote(
                ebuf.at[level, core], ebox.at[slot], s_e.at[level, core], r_e.at[slot], (level, to_core, sy)
            )

        def solve(top):
            def several(turn, error):
                first_level = top - BATCH * turn
                last_level = first_level - BATCH + 1
                arrived(rbuf.at[pl.ds(last_level, BATCH)], r_r.at[last_level // BATCH])
                for n in range(BATCH):
                    whole = rbuf[first_level - n].astype(jnp.int32).astype(F32)
                    unit = jnp.exp2(0.125 * jnp.broadcast_to(whole[:, 0:1], whole.shape)) * (1.0 / WHOLE)
                    dec[n] = whole * unit * keep

                @pl.when(is_end)
                def _():
                    for n in range(BATCH):
                        level = first_level - n
                        arrived(xbuf.at[level], r_rx.at[level])
                        dec[n] = jnp.where(from_extra, unfold(xbuf[level]) * keep, dec[n])

                for n in range(BATCH):
                    level = first_level - n
                    c = [coef[level, i] for i in range(6)]
                    new = c[0] * error + c[1] * roll(error, 64, 1)
                    new = new + (c[2] * roll(error, -1, 0) + c[3] * roll(error, 1, 0))
                    new = new + (c[4] * roll(error, -1, 1) + c[5] * roll(error, 1, 1))
                    error = new + dec[n]
                    for core in range(2):
                        low = new[ROWS * core : ROWS * core + ROWS // 2]
                        high = new[ROWS * core + ROWS // 2 : ROWS * (core + 1)]
                        piece = jnp.where(valid, low, roll(high, 32, 1))
                        ebuf[level, core] = piece
                        if core == 0:
                            ebox[tile] = jnp.where(level == tm, piece, ebox[tile])
                        send_error(level, core).start()
                return error

            return several

        error = lax.fori_loop(0, LEVELS // BATCH, solve(GROUPS - 1), jnp.zeros((2 * ROWS, 128), F32))
        mine[...] = error
        right_tile = lax.rem(tile + 1, TILES)
        left_tile = lax.rem(tile + TILES - 1, TILES)
        right_sy = jnp.where(tile == TILES - 1, east, sy)
        left_sy = jnp.where(tile == 0, west, sy)
        sides = [
            remote(mine, nbr.at[0], s_n.at[0], r_n.at[0], (owner_of(right_tile), 0, right_sy)),
            remote(mine, nbr.at[1], s_n.at[1], r_n.at[1], (owner_of(left_tile), 0, left_sy)),
        ]
        for copy in sides:
            copy.start()
        prepare(0, GROUPS - LEVELS)
        for copy in sides:
            copy.wait_recv()
        error = jnp.where(place < REACH, roll(nbr[0], -32, 1), error)
        error = jnp.where(place >= 64 - REACH, roll(nbr[1], 32, 1), error) * keep
        lax.fori_loop(0, LEVELS // BATCH, solve(GROUPS - LEVELS - 1), error)
        for copy in sides:
            copy.wait_send()

        def wait_errors(level, _):
            for core in range(2):
                send_error(level, core).wait_send()
            return 0

        lax.fori_loop(0, GROUPS, wait_errors, 0)

    def wait_boxes(index, _):
        pl.when(jnp.logical_not(is_owner & (index == tile)))(lambda: arrived(ebox.at[index], r_e.at[index]))
        return 0

    lax.fori_loop(0, TILES, wait_boxes, 0)

    @pl.when((sx == 1) & (lax.rem(x, 2) == lax.rem(z, 2)))
    def _():
        arrived(ebox.at[TILES], r_e.at[TILES])

    lane = iota((ROWS // 2, 128), 1)
    for part in range(2):
        rows = slice(part * ROWS // 2, (part + 1) * ROWS // 2)
        for k in range(2):
            for lane_tile in range(4):
                whole = None
                for i in range(4):
                    piece = roll(ebox[4 * lane_tile + i], 32 * i - REACH - 64 * k - 32 * part, 1)
                    whole = piece if whole is None else jnp.where(lane >= 32 * i, piece, whole)
                lanes = slice(128 * lane_tile, 128 * lane_tile + 128)
                upd[k, rows, lanes] = upd[k, rows, lanes] + whole

    def place_coarse(j, _):
        out[j] = jnp.where(j == here, upd[...], out[j])
        return 0

    lax.fori_loop(0, STEPS, place_coarse, 0)

    for copy in relays:
        copy.wait_send()
    for copy in (*ends(vf, vxbuf, s_v, lambda g: r_vx.at[g]), *ends(rf, xbuf, s_r, lambda g: r_rx.at[g])):
        copy.wait_send()
    to_windows(vw, vbuf, s_v, lambda g: r_v.at[g // LEVELS], False)
    to_windows(rw, rbuf, s_r, lambda g: r_r.at[g // BATCH], False)


def shards(adjoint_guess, sources, velocities, c_points):
    dma = pltpu.SemaphoreType.DMA
    vmem = pl.BlockSpec(memory_space=pltpu.VMEM)
    return pl.pallas_call(
        kernel,
        out_shape=pltpu.VMEM(adjoint_guess.shape, F32),
        in_specs=[pl.BlockSpec(memory_space=pltpu.HBM)] * 4,
        out_specs=vmem,
        scratch_shapes=[
            pltpu.SMEM((GROUPS,), jnp.int32),
            pltpu.VMEM((STEPS, 2, ROWS, COLS), F32),
            pltpu.VMEM((STEPS, 2, ROWS, COLS), jnp.bfloat16),
            pltpu.VMEM((STEPS, 2, XROWS, XCOLS), F32),
            pltpu.VMEM((STEPS, 2, XROWS, XCOLS), F32),
            pltpu.VMEM((2, 2, XROWS, XCOLS), F32),
            pltpu.VMEM((2, 2, XROWS, XCOLS), F32),
            pltpu.VMEM((STEPS, 8, XROWS, XCOLS), F32),
            pltpu.VMEM((2, 3, ROWS, 128), F32),
            pltpu.VMEM((2, 3, XROWS, 128), F32),
            pltpu.VMEM((2, ROWS, 128), F32),
            pltpu.VMEM((2, EDGE, 128), F32),
            pltpu.VMEM((2, ROWS, COLS), jnp.int16),
            pltpu.VMEM((2, ROWS, COLS), jnp.int16),
            pltpu.VMEM((EDGE, 128), F32),
            pltpu.VMEM((EDGE, 128), F32),
            pltpu.VMEM((2, EDGE, 128), F32),
            pltpu.VMEM((2, EDGE, 128), F32),
            pltpu.VMEM((2, ROWS, COLS), F32),
            pltpu.VMEM((2, ROWS, COLS), F32),
            pltpu.VMEM((TILES, ROWS, 128), jnp.int16),
            pltpu.VMEM((2, EDGE, 128), F32),
            pltpu.VMEM((TILES, ROWS, 128), jnp.bfloat16),
            pltpu.VMEM((2, EDGE, 128), F32),
            pltpu.VMEM((GROUPS, 2 * ROWS, 128), jnp.int16),
            pltpu.VMEM((GROUPS, 2 * EDGE, 128), F32),
            pltpu.VMEM((GROUPS, 2 * ROWS, 128), jnp.bfloat16),
            pltpu.VMEM((GROUPS, 2 * EDGE, 128), F32),
            pltpu.VMEM((GROUPS, 6, 2 * ROWS, 128), F32),
            pltpu.VMEM((BATCH, 2 * ROWS, 128), F32),
            pltpu.VMEM((GROUPS, 2, ROWS // 2, 128), F32),
            pltpu.VMEM((TILES + 1, ROWS // 2, 128), F32),
            pltpu.VMEM((2 * ROWS, 128), F32),
            pltpu.VMEM((2, 2 * ROWS, 128), F32),
            dma((7,)), dma((7,)), dma((7,)), dma((7,)),
            dma((TILES + 2,)), dma((GROUPS // LEVELS,)), dma((GROUPS,)),
            dma((TILES + 2,)), dma((GROUPS // BATCH,)), dma((GROUPS,)),
            dma((GROUPS, 2)), dma((TILES + 1,)), dma((2,)), dma((2,)), dma((4,)), pltpu.SemaphoreType.REGULAR,
        ],
        compiler_params=pltpu.CompilerParams(has_side_effects=True, collective_id=0, vmem_limit_bytes=58 * 1024 * 1024),
    )(c_points, adjoint_guess, sources, velocities)


def solution(mesh):
    placed = (P("tm", None, "sx", "sy"), P("tm", None, "sx", "sy"), P("tm", None, "sx", "sy"), P())
    return jax.shard_map(
        shards, mesh=mesh, in_specs=placed, out_specs=P("tm", None, "sx", "sy"), check_vma=False
    )
```

```python
import jax
import jax.numpy as jnp
from jax import lax
from jax.experimental import pallas as pl
from jax.experimental.pallas import tpu as pltpu
from jax.sharding import PartitionSpec as P

F32 = jnp.float32
MESH = pl.DeviceIdType.MESH
STEPS = 8
ROWS = 32
COLS = 512
EDGE = 8
XROWS = ROWS + EDGE
XCOLS = COLS + 128
GROUPS = 32
TILES = 16
WHOLE = 32000.0
REACH = 16
BATCH = 4
LEVELS = 16


def iota(shape, dim):
    return lax.broadcasted_iota(jnp.int32, shape, dim)


def roll(x, shift, dim):
    return pltpu.roll(x, shift % x.shape[dim], dim)


def pack_edges(firsts, lasts):
    lane = iota((ROWS, 128), 1)
    to_west = to_east = jnp.zeros((ROWS, 128), F32)
    for place, (first, last) in enumerate(zip(firsts, lasts)):
        at = EDGE * place
        moved = roll(jnp.where(lane < 64, first(), last()), at, 1)
        to_west = jnp.where(lane // EDGE == place, moved, to_west)
        to_east = jnp.where(lane // EDGE == (place - 1) % 16, moved, to_east)
    return to_west, to_east


def unpack_edges(right, left, place):
    group = iota((XROWS, 128), 1) // EDGE
    return roll(jnp.where(group == place, right, left), -EDGE * place, 1)


def window(read, index):
    lane = iota((ROWS, 128), 1)
    tile, offset = divmod(32 * index - REACH, 128)

    def part(component, target):
        piece = read(component, tile % 4)
        if offset + 64 > 128:
            piece = jnp.where(lane >= offset, piece, read(component, (tile + 1) % 4))
        return roll(piece, target - offset, 1)

    return jnp.where(lane < 64, part(0, 0), part(1, 64))


def fold(part, step):
    lane = lax.rem(iota((EDGE, 128), 1), 64)
    at = 0 if step > 0 else 48
    folded = part[0:EDGE]
    for i in range(1, ROWS // EDGE):
        moved = roll(part[EDGE * i : EDGE * (i + 1)], step * i, 1)
        folded = jnp.where((lane >= at + step * i) & (lane < at + step * i + REACH), moved, folded)
    return folded


def owner_of(tile):
    z = tile // 2
    return z * 4 + 2 * (tile % 2) + z % 2


def kernel(
    c_hbm, guess_hbm, src_hbm, vel_hbm, out,
    c_ref, guess, vel, srcx, velx, fld, nxt, co1, pk, pkr, fp, fpr, fq, nq, fs, ns, ff, nf, res, upd, rw, rf, vw, vf,
    rbuf, xbuf, vbuf, vxbuf, coef, dec, ebuf, ebox, mine, nbr,
    s_a, r_a, s_b, r_b, s_v, r_v, r_vx, s_r, r_r, r_rx, s_e, r_e, s_n, r_n, s_i, known,
):
    tm = lax.axis_index("tm")
    sx = lax.axis_index("sx")
    sy = lax.axis_index("sy")
    east = lax.rem(sy + 1, 4)
    west = lax.rem(sy + 3, 4)
    before = lax.rem(tm + GROUPS - 1, GROUPS)
    edge_row = pl.multiple_of((1 - sx) * (ROWS - EDGE), 8)
    edge = pl.ds(edge_row, EDGE)
    halo = pl.ds(ROWS, EDGE)
    z = tm // 4
    x = lax.rem(tm, 4)
    tile = 2 * z + x // 2
    is_owner = (sx == 0) & (lax.rem(x, 2) == lax.rem(z, 2))
    is_end = is_owner & ((tile == 0) | (tile == TILES - 1))

    def remote(src_ref, dst_ref, send, recv, device):
        return pltpu.make_async_remote_copy(
            src_ref=src_ref, dst_ref=dst_ref, send_sem=send, recv_sem=recv,
            device_id=device, device_id_type=MESH,
        )

    def arrived(ref, sem):
        pltpu.make_async_copy(ref, ref, sem).wait()

    barrier = pltpu.get_barrier_semaphore()

    def greet(*device):
        pl.semaphore_signal(barrier, inc=1, device_id=device, device_id_type=MESH)

    fetch = [
        pltpu.make_async_copy(c_hbm, c_ref, s_i.at[0]),
        pltpu.make_async_copy(vel_hbm, vel, s_i.at[1]),
        pltpu.make_async_copy(src_hbm, srcx.at[:, :, 0:ROWS, 0:COLS], s_i.at[2]),
        pltpu.make_async_copy(guess_hbm, guess, s_i.at[3]),
    ]
    for copy in fetch:
        copy.start()
    column_groups = [lax.rem(tm + 4 * step, GROUPS) for step in range(1, 8)]
    for group in column_groups:
        greet(group, sx, sy)
    for step in range(4):
        group = 4 * z + lax.rem(x + step, 4)
        for core in (sx, 1 - sx):
            for column in (sy, west, east):
                if step > 0 or core is not sx or column is not sy:
                    greet(group, core, column)

    for copy in fetch[:2]:
        copy.wait()
    here = c_ref[tm]

    velx[:, :, 0:ROWS, 0:COLS] = vel[...].astype(F32)
    own = pl.ds(0, COLS)
    head = slice(0, 128)
    tail = slice(COLS - 128, COLS)
    pairs = [(j, k) for j in range(STEPS) for k in range(2)]

    def edges_of(array, count):
        return [[lambda j=j, k=k, lanes=lanes: array[j, k, 0:ROWS, lanes] for j, k in count] for lanes in (head, tail)]

    pk[0, 1], pk[1, 1] = pack_edges(*edges_of(velx, pairs))
    fetch[3].wait()
    fld[0, :, 0:ROWS, 0:COLS] = guess[here]
    pk[0, 2], pk[1, 2] = pack_edges(*edges_of(fld, [(0, 0), (0, 1)]))
    fetch[2].wait()
    pk[0, 0], pk[1, 0] = pack_edges(*edges_of(srcx, pairs))
    copies = [
        remote(srcx.at[:, :, edge, own], srcx.at[:, :, halo, own], s_a.at[0], r_a.at[0], (tm, 1 - sx, sy)),
        remote(velx.at[:, :, edge, own], velx.at[:, :, halo, own], s_a.at[1], r_a.at[1], (tm, 1 - sx, sy)),
        remote(fld.at[0, :, edge, own], fld.at[0, :, halo, own], s_a.at[2], r_a.at[2], (tm, 1 - sx, sy)),
    ]
    for way, target in enumerate((west, east)):
        copies.append(
            remote(pk.at[way], pkr.at[way, :, 0:ROWS], s_a.at[3 + way], r_a.at[3 + way], (tm, sx, target))
        )
        copies.append(
            remote(
                pk.at[way, :, edge], pkr.at[way, :, halo], s_a.at[5 + way], r_a.at[5 + way], (tm, 1 - sx, target)
            )
        )
    pl.semaphore_wait(barrier, 4 * 2 * 3 - 1 + 7)
    for copy in reversed(copies):
        copy.start()

    for group in column_groups:
        pl.semaphore_signal(known, inc=1, device_id=(group, sx, sy), device_id_type=MESH)

    def read_velocity(component, lane_tile):
        return vel[here, component, :, 128 * lane_tile : 128 * lane_tile + 128].astype(F32)

    half = pl.ds(pl.multiple_of(sx * ROWS, ROWS), ROWS)

    eighth = pl.ds(pl.multiple_of(sx * EDGE, EDGE), EDGE)

    def pack_ends(read, folded):
        folded[0] = fold(window(read, -1), -REACH)
        folded[1] = fold(window(read, TILES), REACH)

    def ends(folded, extras, send, recv):
        for side, target, device in ((0, west, owner_of(TILES - 1)), (1, east, owner_of(0))):
            yield remote(folded.at[side], extras.at[tm, eighth], send.at[TILES + side], recv(tm), (device, 0, target))

    def to_windows(source, boxes, send, recv, act):
        for turn in range(TILES):
            index = lax.rem(tile + turn, TILES)
            mine = (owner_of(index) == tm) & (sx == 0)
            slot = jnp.where(mine, GROUPS, tm)
            to_core = jnp.where(mine, 1, 0)
            copy = remote(
                source.at[index], boxes.at[slot, half], send.at[index], recv(slot), (owner_of(index), to_core, sy)
            )
            copy.start() if act else copy.wait_send()
        if act:

            @pl.when(is_owner)
            def _():
                pltpu.make_async_copy(source.at[tile], boxes.at[tm, half], recv(tm)).start()

    def unused_windows(boxes, recv):
        rows = pl.ds(0, ROWS)
        arrived(boxes.at[GROUPS, rows], recv(GROUPS))

    pack_ends(read_velocity, vf)
    for index in range(TILES):
        vw[index] = window(read_velocity, index).astype(jnp.bfloat16)
    out[STEPS - 1] = guess[STEPS - 1]

    pl.semaphore_wait(known, 7)
    for copy in ends(vf, vxbuf, s_v, lambda g: r_vx.at[g]):
        copy.start()
    to_windows(vw, vbuf, s_v, lambda g: r_v.at[g // LEVELS], True)
    for copy in copies:
        copy.wait()
    to_right = jnp.where(sy < 3, 1.0, 0.0).astype(F32)
    to_left = jnp.where(sy > 0, 1.0, 0.0).astype(F32)
    right = [pkr[0, part] * to_right for part in range(3)]
    left = [pkr[1, part] * to_left for part in range(3)]
    for j in range(STEPS):
        for k in range(2):
            srcx[j, k, :, COLS:XCOLS] = unpack_edges(right[0], left[0], 2 * j + k)
            velx[j, k, :, COLS:XCOLS] = unpack_edges(right[1], left[1], 2 * j + k)
    for k in range(2):
        fld[0, k, :, COLS:XCOLS] = unpack_edges(right[2], left[2], k)

    lane = iota((EDGE, XCOLS), 1)
    row = iota((EDGE, XCOLS), 0)
    inside = (lane < COLS) | ((lane < COLS + 64) & (sy < 3)) | ((lane >= COLS + 64) & (sy > 0))
    third = jnp.where(inside, 1.0 / 3.0, 0.0).astype(F32)
    tiles = XROWS // EDGE
    last_own = ROWS // EDGE - 1
    north_ok = jnp.where((row == EDGE - 1) & (sx == 1), 0.0, 1.0).astype(F32)
    south_ok = jnp.where((row == 0) & (sx == 0), 0.0, 1.0).astype(F32)

    def around(parts):
        up = [roll(part, -1, 0) for part in parts]
        down = [roll(part, 1, 0) for part in parts]
        for i, part in enumerate(parts):
            north = jnp.where(row == EDGE - 1, up[(i + 1) % tiles], up[i])
            south = jnp.where(row == 0, down[i - 1], down[i])
            yield part, north, south, roll(part, -1, 1), roll(part, 1, 1)

    def coefficients(j, _):
        u = [velx[j, 0, EDGE * i : EDGE * (i + 1), :] for i in range(tiles)]
        w = [velx[j, 1, EDGE * i : EDGE * (i + 1), :] for i in range(tiles)]
        for i, ((uc, un, us, ue, uw), (wc, wn, ws, we, ww)) in enumerate(zip(around(u), around(w))):
            rows = slice(EDGE * i, EDGE * (i + 1))
            scale_n = scale_s = third
            if i == last_own:
                un, wn, scale_n = un * north_ok, wn * north_ok, third * north_ok
            if i == 0:
                us, ws, scale_s = us * south_ok, ws * south_ok, third * south_ok
            hu, hw = 0.5 * uc, 0.5 * wc
            ht = 0.5 * third
            co1[j, 0, rows] = third - ht * (un - us)
            co1[j, 1, rows] = -ht * (wn - ws)
            co1[j, 2, rows] = third - ht * (we - ww)
            co1[j, 3, rows] = -ht * (ue - uw)
            co1[j, 4, rows] = scale_n * (0.5 + hu)
            co1[j, 5, rows] = scale_s * (0.5 - hu)
            co1[j, 6, rows] = third * (0.5 + hw)
            co1[j, 7, rows] = third * (0.5 - hw)
        return 0

    lax.fori_loop(0, STEPS - 1, coefficients, 0)

    def phi(field, slot, j):
        p = [field[slot, 0, EDGE * i : EDGE * (i + 1), :] for i in range(tiles)]
        q = [field[slot, 1, EDGE * i : EDGE * (i + 1), :] for i in range(tiles)]
        for i, ((pc, pn, ps, pe, pw), (qc, qn, qs, qe, qw)) in enumerate(zip(around(p), around(q))):
            rows = slice(EDGE * i, EDGE * (i + 1))
            a = [co1[j, n, rows] for n in range(8)]
            new_p = a[0] * pc + a[1] * qc + a[4] * pn + a[5] * ps + a[6] * pe + a[7] * pw + srcx[j, 0, rows]
            new_q = a[2] * qc + a[3] * pc + a[4] * qn + a[5] * qs + a[6] * qe + a[7] * qw + srcx[j, 1, rows]
            yield rows, i, ((0, pc, new_p), (1, qc, new_q))

    def lower(turn, _):
        j = STEPS - 2 - turn
        slot = lax.rem(turn, 2)
        active = j < here
        for rows, i, parts in phi(fld, slot, j):
            for k, old, new in parts:
                fld[1 - slot, k, rows] = jnp.where(active, new, old)
                if i <= last_own:
                    out[j, k, rows] = new[:, 0:COLS]
        return 0

    lax.fori_loop(0, STEPS - 1, lower, 0)
    done = (STEPS - 1) % 2

    largest = jnp.max(jnp.abs(fld[done, :, 0:ROWS, 0:COLS]), axis=(0, 2))[:, None]
    power = jnp.floor(8.0 * jnp.log2(jnp.maximum(largest, 1e-30))) + 2.0
    to_unit = WHOLE * jnp.exp2(-0.125 * power)
    for k in range(2):
        fq[k] = jnp.floor(fld[done, k, 0:ROWS, 0:COLS] * to_unit + 0.5).astype(jnp.int32).astype(jnp.int16)
    quarter = iota((EDGE, 128), 1) // 32
    spread = jnp.broadcast_to(power, (ROWS, 128))
    scales = spread[0:EDGE]
    for i in range(1, ROWS // EDGE):
        scales = jnp.where(quarter == i, spread[EDGE * i : EDGE * (i + 1)], scales)
    fs[...] = scales
    relays = [
        remote(fld.at[done, :, edge, own], nxt.at[0, :, halo, own], s_b.at[1], r_b.at[1], (before, 1 - sx, sy)),
        remote(fq, nq, s_b.at[0], r_b.at[0], (before, sx, sy)),
        remote(fs, ns, s_b.at[6], r_b.at[6], (before, sx, sy)),
    ]
    fp[0], fp[1] = pack_edges(*edges_of(fld, [(done, 0), (done, 1)]))
    for way, target in enumerate((west, east)):
        sixteenth = iota((EDGE, 128), 1) // (2 * EDGE)
        folded = roll(fp[way, 0:EDGE], EDGE * way, 1)
        for i in range(1, ROWS // EDGE):
            moved = roll(fp[way, EDGE * i : EDGE * (i + 1)], EDGE * (2 * i + way), 1)
            folded = jnp.where(sixteenth == i, moved, folded)
        ff[way] = folded
        relays.append(remote(ff.at[way], nf.at[way], s_b.at[2 + way], r_b.at[2 + way], (before, sx, target)))
        relays.append(
            remote(fp.at[way, edge], fpr.at[way], s_b.at[4 + way], r_b.at[4 + way], (before, 1 - sx, target))
        )
    for copy in reversed(relays):
        copy.start()
    coefficients(STEPS - 1, 0)

    for copy in relays:
        copy.wait_recv()
    got = [
        jnp.concatenate([roll(nf[way], -EDGE * (2 * i + way), 1) for i in range(ROWS // EDGE)] + [fpr[way]], 0)
        for way in range(2)
    ]
    for k in range(2):
        nxt[0, k, :, COLS:XCOLS] = unpack_edges(got[0] * to_right, got[1] * to_left, k)
    scales = ns[...]
    unit = jnp.concatenate(
        [jnp.broadcast_to(scales[:, 32 * i : 32 * i + 1], (EDGE, 128)) for i in range(ROWS // EDGE)], 0
    )
    unit = jnp.exp2(0.125 * unit) * (1.0 / WHOLE)
    for k in range(2):
        for lane_tile in range(COLS // 128):
            lanes = slice(128 * lane_tile, 128 * lane_tile + 128)
            nxt[0, k, 0:ROWS, lanes] = nq[k, :, lanes].astype(jnp.int32).astype(F32) * unit

    @pl.when(tm == GROUPS - 1)
    def _():
        nxt[0] = jnp.zeros((2, XROWS, XCOLS), F32)

    def upper(turn, _):
        j = STEPS - 1 - turn
        slot = lax.rem(turn, 2)
        above = j > here
        coarse = j == here
        for rows, i, parts in phi(nxt, slot, j):
            for k, old, new in parts:
                nxt[1 - slot, k, rows] = jnp.where(above, new, old)
                if i <= last_own:
                    inner = new[:, 0:COLS]
                    out[j, k, rows] = jnp.where(above, inner, out[j, k, rows])
                    upd[k, rows] = jnp.where(coarse, inner, upd[k, rows])
        return 0

    upd[...] = jnp.zeros((2, ROWS, COLS), F32)
    lax.fori_loop(0, STEPS, upper, 0)

    res[...] = upd[...] - guess[here]

    def read_residual(component, lane_tile):
        return res[component, :, 128 * lane_tile : 128 * lane_tile + 128]

    pack_ends(read_residual, rf)
    for copy in ends(rf, xbuf, s_r, lambda g: r_rx.at[g]):
        copy.start()
    largest = jnp.max(jnp.abs(res[...]), axis=(0, 2))[:, None]
    power = jnp.floor(8.0 * jnp.log2(jnp.maximum(largest, 1e-30))) + 2.0
    power = jnp.broadcast_to(power, (ROWS, 128))
    to_unit = WHOLE * jnp.exp2(-0.125 * power)
    first_lane = iota((ROWS, 128), 1) == 0
    for index in range(TILES):
        piece = jnp.floor(window(read_residual, index) * to_unit + 0.5)
        rw[index] = jnp.where(first_lane, power, piece).astype(jnp.int32).astype(jnp.int16)
    to_windows(rw, rbuf, s_r, lambda g: r_r.at[g // BATCH], True)

    def send_error(level, core):
        own = (level == tm) & (core == 0)
        slot = jnp.where(own, TILES, tile)
        to_core = jnp.where(own, 1, core)
        return remote(
            ebuf.at[level, core], ebox.at[slot], s_e.at[level, core], r_e.at[slot], (level, to_core, sy)
        )

    right_tile = lax.rem(tile + 1, TILES)
    left_tile = lax.rem(tile + TILES - 1, TILES)
    right_sy = jnp.where(tile == TILES - 1, east, sy)
    left_sy = jnp.where(tile == 0, west, sy)
    refresh = [
        remote(mine, nbr.at[0], s_n.at[0], r_n.at[0], (owner_of(right_tile), 0, right_sy)),
        remote(mine, nbr.at[1], s_n.at[1], r_n.at[1], (owner_of(left_tile), 0, left_sy)),
    ]

    window_lane = iota((2 * ROWS, 128), 1)
    grid_row = iota((2 * ROWS, 128), 0)
    place = lax.rem(window_lane, 64)
    first = window_lane < 64
    from_extra = ((place < REACH) & (tile == 0)) | ((place >= 64 - REACH) & (tile == TILES - 1))
    outside = ((place < REACH) & (tile == 0) & (sy == 0)) | (
        (place >= 64 - REACH) & (tile == TILES - 1) & (sy == 3)
    )
    valid = (place[0 : ROWS // 2] >= REACH) & (place[0 : ROWS // 2] < 64 - REACH)
    keep = jnp.where(outside, 0.0, 1.0).astype(F32)
    top_open = jnp.where(grid_row == 2 * ROWS - 1, 0.0, 1.0).astype(F32)
    bottom_open = jnp.where(grid_row == 0, 0.0, 1.0).astype(F32)

    def unfold(part):
        pieces = [part[EDGE * core : EDGE * (core + 1)] for core in range(2)]
        step = jnp.where(tile == 0, 128 - REACH, REACH)
        return jnp.concatenate(
            [pltpu.roll(piece, lax.rem(step * i, 128), 1) for piece in pieces for i in range(ROWS // EDGE)], 0
        )

    @pl.when(is_owner)
    def _():
        def merge(level, _):
            arrived(vxbuf.at[level], r_vx.at[level])
            both = jnp.where(from_extra, unfold(vxbuf[level]), vbuf[level].astype(F32))
            vbuf[level] = both.astype(jnp.bfloat16)
            return 0

        def coarse_coefficients(level, _):
            v = vbuf[level].astype(F32) * keep
            after = jnp.where(level + 1 < GROUPS, c_ref[jnp.minimum(level + 1, GROUPS - 1)], 0)
            span = jnp.full((1, 128), STEPS + after - c_ref[level], jnp.int32).astype(F32)
            inverse = keep * (1.0 / (1.0 + 2.0 * span))
            k = span * inverse
            swapped = roll(v, 64, 1)
            u = jnp.where(first, v, swapped)
            w = jnp.where(first, swapped, v)
            dx = 0.5 * (roll(v, -1, 0) * top_open - roll(v, 1, 0) * bottom_open)
            dy = 0.5 * (roll(v, -1, 1) - roll(v, 1, 1))
            coef[level, 0] = inverse - k * jnp.where(first, dx, dy)
            coef[level, 1] = -k * jnp.where(first, roll(dx, 64, 1), roll(dy, 64, 1))
            coef[level, 2] = k * (0.5 + 0.5 * u) * top_open
            coef[level, 3] = k * (0.5 - 0.5 * u) * bottom_open
            coef[level, 4] = k * (0.5 + 0.5 * w)
            coef[level, 5] = k * (0.5 - 0.5 * w)
            return 0

        def prepare(low, high):
            arrived(vbuf.at[low:high], r_v.at[low // LEVELS])

            @pl.when(is_end)
            def _():
                lax.fori_loop(low, high, merge, 0)

            lax.fori_loop(low, high, coarse_coefficients, 0)

        prepare(GROUPS - LEVELS, GROUPS)

        def solve(top):
            def several(turn, error):
                first_level = top - BATCH * turn
                last_level = first_level - BATCH + 1
                arrived(rbuf.at[pl.ds(last_level, BATCH)], r_r.at[last_level // BATCH])
                for n in range(BATCH):
                    whole = rbuf[first_level - n].astype(jnp.int32).astype(F32)
                    unit = jnp.exp2(0.125 * jnp.broadcast_to(whole[:, 0:1], whole.shape)) * (1.0 / WHOLE)
                    dec[n] = whole * unit * keep

                @pl.when(is_end)
                def _():
                    for n in range(BATCH):
                        level = first_level - n
                        arrived(xbuf.at[level], r_rx.at[level])
                        dec[n] = jnp.where(from_extra, unfold(xbuf[level]) * keep, dec[n])

                for n in range(BATCH):
                    level = first_level - n
                    c = [coef[level, i] for i in range(6)]
                    new = c[0] * error + c[1] * roll(error, 64, 1)
                    new = new + (c[2] * roll(error, -1, 0) + c[3] * roll(error, 1, 0))
                    new = new + (c[4] * roll(error, -1, 1) + c[5] * roll(error, 1, 1))
                    error = new + dec[n]
                    for core in range(2):
                        low = new[ROWS * core : ROWS * core + ROWS // 2]
                        high = new[ROWS * core + ROWS // 2 : ROWS * (core + 1)]
                        piece = jnp.where(valid, low, roll(high, 32, 1))
                        ebuf[level, core] = piece
                        if core == 0:
                            ebox[tile] = jnp.where(level == tm, piece, ebox[tile])
                        send_error(level, core).start()
                return error

            return several

        error = lax.fori_loop(0, LEVELS // BATCH, solve(GROUPS - 1), jnp.zeros((2 * ROWS, 128), F32))
        mine[...] = error
        for copy in refresh:
            copy.start()
        prepare(0, GROUPS - LEVELS)
        for copy in refresh:
            copy.wait_recv()
        error = jnp.where(place < REACH, roll(nbr[0], -32, 1), error)
        error = jnp.where(place >= 64 - REACH, roll(nbr[1], 32, 1), error) * keep
        lax.fori_loop(0, LEVELS // BATCH, solve(GROUPS - LEVELS - 1), error)

    for copy in relays:
        copy.wait_send()
    for copy in (*ends(vf, vxbuf, s_v, lambda g: r_vx.at[g]), *ends(rf, xbuf, s_r, lambda g: r_rx.at[g])):
        copy.wait_send()
    to_windows(vw, vbuf, s_v, lambda g: r_v.at[g // LEVELS], False)
    to_windows(rw, rbuf, s_r, lambda g: r_r.at[g // BATCH], False)
    owner_chip = lax.rem(x, 2) == lax.rem(z, 2)

    @pl.when((sx == 1) & owner_chip)
    def _():
        unused_windows(vbuf, lambda g: r_v.at[g // LEVELS])
        unused_windows(rbuf, lambda g: r_r.at[g // BATCH])

    def wait_boxes(index, _):
        pl.when(jnp.logical_not(is_owner & (index == tile)))(lambda: arrived(ebox.at[index], r_e.at[index]))
        return 0

    lax.fori_loop(0, TILES, wait_boxes, 0)

    @pl.when((sx == 1) & owner_chip)
    def _():
        arrived(ebox.at[TILES], r_e.at[TILES])

    lane = iota((ROWS // 2, 128), 1)
    for part in range(2):
        rows = slice(part * ROWS // 2, (part + 1) * ROWS // 2)
        for k in range(2):
            for lane_tile in range(4):
                whole = None
                for i in range(4):
                    piece = roll(ebox[4 * lane_tile + i], 32 * i - REACH - 64 * k - 32 * part, 1)
                    whole = piece if whole is None else jnp.where(lane >= 32 * i, piece, whole)
                lanes = slice(128 * lane_tile, 128 * lane_tile + 128)
                upd[k, rows, lanes] = upd[k, rows, lanes] + whole

    def place_coarse(j, _):
        out[j] = jnp.where(j == here, upd[...], out[j])
        return 0

    lax.fori_loop(0, STEPS, place_coarse, 0)

    @pl.when(is_owner)
    def _():
        for copy in refresh:
            copy.wait_send()

        def wait_errors(level, _):
            for core in range(2):
                send_error(level, core).wait_send()
            return 0

        lax.fori_loop(0, GROUPS, wait_errors, 0)


def shards(adjoint_guess, sources, velocities, c_points):
    dma = pltpu.SemaphoreType.DMA
    vmem = pl.BlockSpec(memory_space=pltpu.VMEM)
    return pl.pallas_call(
        kernel,
        out_shape=pltpu.VMEM(adjoint_guess.shape, F32),
        in_specs=[pl.BlockSpec(memory_space=pltpu.HBM)] * 4,
        out_specs=vmem,
        scratch_shapes=[
            pltpu.SMEM((GROUPS,), jnp.int32),
            pltpu.VMEM((STEPS, 2, ROWS, COLS), F32),
            pltpu.VMEM((STEPS, 2, ROWS, COLS), jnp.bfloat16),
            pltpu.VMEM((STEPS, 2, XROWS, XCOLS), F32),
            pltpu.VMEM((STEPS, 2, XROWS, XCOLS), F32),
            pltpu.VMEM((2, 2, XROWS, XCOLS), F32),
            pltpu.VMEM((2, 2, XROWS, XCOLS), F32),
            pltpu.VMEM((STEPS, 8, XROWS, XCOLS), F32),
            pltpu.VMEM((2, 3, ROWS, 128), F32),
            pltpu.VMEM((2, 3, XROWS, 128), F32),
            pltpu.VMEM((2, ROWS, 128), F32),
            pltpu.VMEM((2, EDGE, 128), F32),
            pltpu.VMEM((2, ROWS, COLS), jnp.int16),
            pltpu.VMEM((2, ROWS, COLS), jnp.int16),
            pltpu.VMEM((EDGE, 128), F32),
            pltpu.VMEM((EDGE, 128), F32),
            pltpu.VMEM((2, EDGE, 128), F32),
            pltpu.VMEM((2, EDGE, 128), F32),
            pltpu.VMEM((2, ROWS, COLS), F32),
            pltpu.VMEM((2, ROWS, COLS), F32),
            pltpu.VMEM((TILES, ROWS, 128), jnp.int16),
            pltpu.VMEM((2, EDGE, 128), F32),
            pltpu.VMEM((TILES, ROWS, 128), jnp.bfloat16),
            pltpu.VMEM((2, EDGE, 128), F32),
            pltpu.VMEM((GROUPS + 1, 2 * ROWS, 128), jnp.int16),
            pltpu.VMEM((GROUPS, 2 * EDGE, 128), F32),
            pltpu.VMEM((GROUPS + 1, 2 * ROWS, 128), jnp.bfloat16),
            pltpu.VMEM((GROUPS, 2 * EDGE, 128), F32),
            pltpu.VMEM((GROUPS, 6, 2 * ROWS, 128), F32),
            pltpu.VMEM((BATCH, 2 * ROWS, 128), F32),
            pltpu.VMEM((GROUPS, 2, ROWS // 2, 128), F32),
            pltpu.VMEM((TILES + 1, ROWS // 2, 128), F32),
            pltpu.VMEM((2 * ROWS, 128), F32),
            pltpu.VMEM((2, 2 * ROWS, 128), F32),
            dma((7,)), dma((7,)), dma((7,)), dma((7,)),
            dma((TILES + 2,)), dma((GROUPS // LEVELS + 1,)), dma((GROUPS,)),
            dma((TILES + 2,)), dma((GROUPS // BATCH + 1,)), dma((GROUPS,)),
            dma((GROUPS, 2)), dma((TILES + 1,)), dma((2,)), dma((2,)), dma((4,)), pltpu.SemaphoreType.REGULAR,
        ],
        compiler_params=pltpu.CompilerParams(has_side_effects=True, collective_id=0, vmem_limit_bytes=58 * 1024 * 1024),
    )(c_points, adjoint_guess, sources, velocities)


def solution(mesh):
    placed = (P("tm", None, "sx", "sy"), P("tm", None, "sx", "sy"), P("tm", None, "sx", "sy"), P())
    return jax.shard_map(
        shards, mesh=mesh, in_specs=placed, out_specs=P("tm", None, "sx", "sy"), check_vma=False
    )
```

```python
import functools

import jax
import jax.numpy as jnp
from jax import lax
from jax.experimental import pallas as pl
from jax.experimental.pallas import tpu as pltpu
from jax.sharding import PartitionSpec as P

F32 = jnp.float32
MESH = pl.DeviceIdType.MESH
STEPS = 8
ROWS = 32
COLS = 512
EDGE = 8
XROWS = ROWS + EDGE
XCOLS = COLS + 128
GROUPS = 32
TILES = 16
WHOLE = 32000.0
REACH = 16
BATCH = 4
LEVELS = 16


def iota(shape, dim):
    return lax.broadcasted_iota(jnp.int32, shape, dim)


def roll(x, shift, dim):
    return pltpu.roll(x, shift % x.shape[dim], dim)


def pack_edges(firsts, lasts):
    lane = iota((ROWS, 128), 1)
    to_west = to_east = jnp.zeros((ROWS, 128), F32)
    for place, (first, last) in enumerate(zip(firsts, lasts)):
        at = EDGE * place
        moved = roll(jnp.where(lane < 64, first(), last()), at, 1)
        to_west = jnp.where(lane // EDGE == place, moved, to_west)
        to_east = jnp.where(lane // EDGE == (place - 1) % 16, moved, to_east)
    return to_west, to_east


def unpack_edges(right, left, place):
    group = iota((XROWS, 128), 1) // EDGE
    return roll(jnp.where(group == place, right, left), -EDGE * place, 1)


def window(read, index):
    lane = iota((ROWS, 128), 1)
    tile, offset = divmod(32 * index - REACH, 128)

    def part(component, target):
        piece = read(component, tile % 4)
        if offset + 64 > 128:
            piece = jnp.where(lane >= offset, piece, read(component, (tile + 1) % 4))
        return roll(piece, target - offset, 1)

    return jnp.where(lane < 64, part(0, 0), part(1, 64))


def fold(part, step):
    lane = lax.rem(iota((EDGE, 128), 1), 64)
    at = 0 if step > 0 else 48
    folded = part[0:EDGE]
    for i in range(1, ROWS // EDGE):
        moved = roll(part[EDGE * i : EDGE * (i + 1)], step * i, 1)
        folded = jnp.where((lane >= at + step * i) & (lane < at + step * i + REACH), moved, folded)
    return folded


def owner_of(tile):
    z = tile // 2
    return z * 4 + 2 * (tile % 2) + z % 2


def kernel(
    c_hbm, guess_hbm, src_hbm, vel_hbm, out,
    c_ref, guess, vel, srcx, velx, fld, nxt, co1, pk, pkr, fp, fpr, fq, nq, fs, ns, ff, nf, res, upd, rw, rf, vw, vf,
    rbuf, xbuf, vbuf, vxbuf, coef, dec, ebuf, ebox, mine, nbr,
    s_a, r_a, s_b, r_b, s_v, r_v, r_vx, s_r, r_r, r_rx, s_e, r_e, s_n, r_n, s_i, known,
):
    tm = lax.axis_index("tm")
    sx = lax.axis_index("sx")
    sy = lax.axis_index("sy")
    east = lax.rem(sy + 1, 4)
    west = lax.rem(sy + 3, 4)
    before = lax.rem(tm + GROUPS - 1, GROUPS)
    edge_row = pl.multiple_of((1 - sx) * (ROWS - EDGE), 8)
    edge = pl.ds(edge_row, EDGE)
    halo = pl.ds(ROWS, EDGE)
    z = tm // 4
    x = lax.rem(tm, 4)
    tile = 2 * z + x // 2
    is_owner = (sx == 0) & (lax.rem(x, 2) == lax.rem(z, 2))
    is_end = is_owner & ((tile == 0) | (tile == TILES - 1))

    def remote(src_ref, dst_ref, send, recv, device):
        return pltpu.make_async_remote_copy(
            src_ref=src_ref, dst_ref=dst_ref, send_sem=send, recv_sem=recv,
            device_id=device, device_id_type=MESH,
        )

    def arrived(ref, sem):
        pltpu.make_async_copy(ref, ref, sem).wait()

    barrier = pltpu.get_barrier_semaphore()

    def greet(*device):
        pl.semaphore_signal(barrier, inc=1, device_id=device, device_id_type=MESH)

    fetch = [
        pltpu.make_async_copy(c_hbm, c_ref, s_i.at[0]),
        pltpu.make_async_copy(vel_hbm, vel, s_i.at[1]),
        pltpu.make_async_copy(src_hbm, srcx.at[:, :, 0:ROWS, 0:COLS], s_i.at[2]),
        pltpu.make_async_copy(guess_hbm, guess, s_i.at[3]),
    ]
    for copy in fetch:
        copy.start()
    column_groups = [lax.rem(tm + 4 * step, GROUPS) for step in range(1, 8)]
    for group in column_groups:
        greet(group, sx, sy)
    for step in range(4):
        group = 4 * z + lax.rem(x + step, 4)
        for core in (sx, 1 - sx):
            for column in (sy, west, east):
                if step > 0 or core is not sx or column is not sy:
                    greet(group, core, column)

    for copy in fetch[:2]:
        copy.wait()
    here = c_ref[tm]

    velx[:, :, 0:ROWS, 0:COLS] = vel[...].astype(F32)
    own = pl.ds(0, COLS)
    head = slice(0, 128)
    tail = slice(COLS - 128, COLS)
    pairs = [(j, k) for j in range(STEPS) for k in range(2)]

    def edges_of(array, count):
        return [[lambda j=j, k=k, lanes=lanes: array[j, k, 0:ROWS, lanes] for j, k in count] for lanes in (head, tail)]

    pk[0, 1], pk[1, 1] = pack_edges(*edges_of(velx, pairs))
    fetch[3].wait()
    fld[0, :, 0:ROWS, 0:COLS] = guess[here]
    pk[0, 2], pk[1, 2] = pack_edges(*edges_of(fld, [(0, 0), (0, 1)]))
    fetch[2].wait()
    pk[0, 0], pk[1, 0] = pack_edges(*edges_of(srcx, pairs))
    copies = [
        remote(srcx.at[:, :, edge, own], srcx.at[:, :, halo, own], s_a.at[0], r_a.at[0], (tm, 1 - sx, sy)),
        remote(velx.at[:, :, edge, own], velx.at[:, :, halo, own], s_a.at[1], r_a.at[1], (tm, 1 - sx, sy)),
        remote(fld.at[0, :, edge, own], fld.at[0, :, halo, own], s_a.at[2], r_a.at[2], (tm, 1 - sx, sy)),
    ]
    for way, target in enumerate((west, east)):
        copies.append(
            remote(pk.at[way], pkr.at[way, :, 0:ROWS], s_a.at[3 + way], r_a.at[3 + way], (tm, sx, target))
        )
        copies.append(
            remote(
                pk.at[way, :, edge], pkr.at[way, :, halo], s_a.at[5 + way], r_a.at[5 + way], (tm, 1 - sx, target)
            )
        )
    pl.semaphore_wait(barrier, 4 * 2 * 3 - 1 + 7)
    for copy in reversed(copies):
        copy.start()

    for group in column_groups:
        pl.semaphore_signal(known, inc=1, device_id=(group, sx, sy), device_id_type=MESH)

    def read_velocity(component, lane_tile):
        return vel[here, component, :, 128 * lane_tile : 128 * lane_tile + 128].astype(F32)

    half = pl.ds(pl.multiple_of(sx * ROWS, ROWS), ROWS)

    eighth = pl.ds(pl.multiple_of(sx * EDGE, EDGE), EDGE)

    def pack_ends(read, folded):
        folded[0] = fold(window(read, -1), -REACH)
        folded[1] = fold(window(read, TILES), REACH)

    def ends(folded, extras, send, recv):
        for side, target, device in ((0, west, owner_of(TILES - 1)), (1, east, owner_of(0))):
            yield remote(folded.at[side], extras.at[tm, eighth], send.at[TILES + side], recv(tm), (device, 0, target))

    def to_windows(source, boxes, send, recv, act):
        for turn in range(TILES):
            index = lax.rem(tile + turn, TILES)
            mine = (owner_of(index) == tm) & (sx == 0)
            slot = jnp.where(mine, GROUPS, tm)
            to_core = jnp.where(mine, 1, 0)
            copy = remote(
                source.at[index], boxes.at[slot, half], send.at[index], recv(slot), (owner_of(index), to_core, sy)
            )
            copy.start() if act else copy.wait_send()
        if act:

            @pl.when(is_owner)
            def _():
                pltpu.make_async_copy(source.at[tile], boxes.at[tm, half], recv(tm)).start()

    def unused_windows(boxes, recv):
        rows = pl.ds(0, ROWS)
        arrived(boxes.at[GROUPS, rows], recv(GROUPS))

    pack_ends(read_velocity, vf)
    for index in range(TILES):
        vw[index] = window(read_velocity, index).astype(jnp.bfloat16)
    out[STEPS - 1] = guess[STEPS - 1]

    pl.semaphore_wait(known, 7)
    for copy in ends(vf, vxbuf, s_v, lambda g: r_vx.at[g]):
        copy.start()
    to_windows(vw, vbuf, s_v, lambda g: r_v.at[g // LEVELS], True)
    for copy in copies:
        copy.wait()
    to_right = jnp.where(sy < 3, 1.0, 0.0).astype(F32)
    to_left = jnp.where(sy > 0, 1.0, 0.0).astype(F32)
    right = [pkr[0, part] * to_right for part in range(3)]
    left = [pkr[1, part] * to_left for part in range(3)]
    for j in range(STEPS):
        for k in range(2):
            srcx[j, k, :, COLS:XCOLS] = unpack_edges(right[0], left[0], 2 * j + k)
            velx[j, k, :, COLS:XCOLS] = unpack_edges(right[1], left[1], 2 * j + k)
    for k in range(2):
        fld[0, k, :, COLS:XCOLS] = unpack_edges(right[2], left[2], k)

    lane = iota((EDGE, XCOLS), 1)
    row = iota((EDGE, XCOLS), 0)
    inside = (lane < COLS) | ((lane < COLS + 64) & (sy < 3)) | ((lane >= COLS + 64) & (sy > 0))
    third = jnp.where(inside, 1.0 / 3.0, 0.0).astype(F32)
    tiles = XROWS // EDGE
    last_own = ROWS // EDGE - 1
    north_ok = jnp.where((row == EDGE - 1) & (sx == 1), 0.0, 1.0).astype(F32)
    south_ok = jnp.where((row == 0) & (sx == 0), 0.0, 1.0).astype(F32)

    def around(parts):
        up = [roll(part, -1, 0) for part in parts]
        down = [roll(part, 1, 0) for part in parts]
        for i, part in enumerate(parts):
            north = jnp.where(row == EDGE - 1, up[(i + 1) % tiles], up[i])
            south = jnp.where(row == 0, down[i - 1], down[i])
            yield part, north, south, roll(part, -1, 1), roll(part, 1, 1)

    def coefficients(j, _):
        u = [velx[j, 0, EDGE * i : EDGE * (i + 1), :] for i in range(tiles)]
        w = [velx[j, 1, EDGE * i : EDGE * (i + 1), :] for i in range(tiles)]
        for i, ((uc, un, us, ue, uw), (wc, wn, ws, we, ww)) in enumerate(zip(around(u), around(w))):
            rows = slice(EDGE * i, EDGE * (i + 1))
            scale_n = scale_s = third
            if i == last_own:
                un, wn, scale_n = un * north_ok, wn * north_ok, third * north_ok
            if i == 0:
                us, ws, scale_s = us * south_ok, ws * south_ok, third * south_ok
            hu, hw = 0.5 * uc, 0.5 * wc
            ht = 0.5 * third
            co1[j, 0, rows] = third - ht * (un - us)
            co1[j, 1, rows] = -ht * (wn - ws)
            co1[j, 2, rows] = third - ht * (we - ww)
            co1[j, 3, rows] = -ht * (ue - uw)
            co1[j, 4, rows] = scale_n * (0.5 + hu)
            co1[j, 5, rows] = scale_s * (0.5 - hu)
            co1[j, 6, rows] = third * (0.5 + hw)
            co1[j, 7, rows] = third * (0.5 - hw)
        return 0

    lax.fori_loop(0, STEPS - 1, coefficients, 0)

    def phi(field, slot, j):
        p = [field[slot, 0, EDGE * i : EDGE * (i + 1), :] for i in range(tiles)]
        q = [field[slot, 1, EDGE * i : EDGE * (i + 1), :] for i in range(tiles)]
        for i, ((pc, pn, ps, pe, pw), (qc, qn, qs, qe, qw)) in enumerate(zip(around(p), around(q))):
            rows = slice(EDGE * i, EDGE * (i + 1))
            a = [co1[j, n, rows] for n in range(8)]
            new_p = a[0] * pc + a[1] * qc + a[4] * pn + a[5] * ps + a[6] * pe + a[7] * pw + srcx[j, 0, rows]
            new_q = a[2] * qc + a[3] * pc + a[4] * qn + a[5] * qs + a[6] * qe + a[7] * qw + srcx[j, 1, rows]
            yield rows, i, ((0, pc, new_p), (1, qc, new_q))

    def lower(turn, _):
        j = STEPS - 2 - turn
        slot = lax.rem(turn, 2)
        active = j < here
        for rows, i, parts in phi(fld, slot, j):
            for k, old, new in parts:
                fld[1 - slot, k, rows] = jnp.where(active, new, old)
                if i <= last_own:
                    out[j, k, rows] = new[:, 0:COLS]
        return 0

    lax.fori_loop(0, STEPS - 1, lower, 0)
    done = (STEPS - 1) % 2

    largest = jnp.max(jnp.abs(fld[done, :, 0:ROWS, 0:COLS]), axis=(0, 2))[:, None]
    power = jnp.floor(8.0 * jnp.log2(jnp.maximum(largest, 1e-30))) + 2.0
    to_unit = WHOLE * jnp.exp2(-0.125 * power)
    for k in range(2):
        fq[k] = jnp.floor(fld[done, k, 0:ROWS, 0:COLS] * to_unit + 0.5).astype(jnp.int32).astype(jnp.int16)
    quarter = iota((EDGE, 128), 1) // 32
    spread = jnp.broadcast_to(power, (ROWS, 128))
    scales = spread[0:EDGE]
    for i in range(1, ROWS // EDGE):
        scales = jnp.where(quarter == i, spread[EDGE * i : EDGE * (i + 1)], scales)
    fs[...] = scales
    relays = [
        remote(fld.at[done, :, edge, own], nxt.at[0, :, halo, own], s_b.at[1], r_b.at[1], (before, 1 - sx, sy)),
        remote(fq, nq, s_b.at[0], r_b.at[0], (before, sx, sy)),
        remote(fs, ns, s_b.at[6], r_b.at[6], (before, sx, sy)),
    ]
    fp[0], fp[1] = pack_edges(*edges_of(fld, [(done, 0), (done, 1)]))
    for way, target in enumerate((west, east)):
        sixteenth = iota((EDGE, 128), 1) // (2 * EDGE)
        folded = roll(fp[way, 0:EDGE], EDGE * way, 1)
        for i in range(1, ROWS // EDGE):
            moved = roll(fp[way, EDGE * i : EDGE * (i + 1)], EDGE * (2 * i + way), 1)
            folded = jnp.where(sixteenth == i, moved, folded)
        ff[way] = folded
        relays.append(remote(ff.at[way], nf.at[way], s_b.at[2 + way], r_b.at[2 + way], (before, sx, target)))
        relays.append(
            remote(fp.at[way, edge], fpr.at[way], s_b.at[4 + way], r_b.at[4 + way], (before, 1 - sx, target))
        )
    for copy in reversed(relays):
        copy.start()
    coefficients(STEPS - 1, 0)

    for copy in relays:
        copy.wait_recv()
    got = [
        jnp.concatenate([roll(nf[way], -EDGE * (2 * i + way), 1) for i in range(ROWS // EDGE)] + [fpr[way]], 0)
        for way in range(2)
    ]
    for k in range(2):
        nxt[0, k, :, COLS:XCOLS] = unpack_edges(got[0] * to_right, got[1] * to_left, k)
    scales = ns[...]
    unit = jnp.concatenate(
        [jnp.broadcast_to(scales[:, 32 * i : 32 * i + 1], (EDGE, 128)) for i in range(ROWS // EDGE)], 0
    )
    unit = jnp.exp2(0.125 * unit) * (1.0 / WHOLE)
    for k in range(2):
        for lane_tile in range(COLS // 128):
            lanes = slice(128 * lane_tile, 128 * lane_tile + 128)
            nxt[0, k, 0:ROWS, lanes] = nq[k, :, lanes].astype(jnp.int32).astype(F32) * unit

    @pl.when(tm == GROUPS - 1)
    def _():
        nxt[0] = jnp.zeros((2, XROWS, XCOLS), F32)

    def upper(turn, _):
        j = STEPS - 1 - turn
        slot = lax.rem(turn, 2)
        above = j > here
        coarse = j == here
        for rows, i, parts in phi(nxt, slot, j):
            for k, old, new in parts:
                nxt[1 - slot, k, rows] = jnp.where(above, new, old)
                if i <= last_own:
                    inner = new[:, 0:COLS]
                    out[j, k, rows] = jnp.where(above, inner, out[j, k, rows])
                    upd[k, rows] = jnp.where(coarse, inner, upd[k, rows])
        return 0

    upd[...] = jnp.zeros((2, ROWS, COLS), F32)
    lax.fori_loop(0, STEPS, upper, 0)

    res[...] = upd[...] - guess[here]

    def read_residual(component, lane_tile):
        return res[component, :, 128 * lane_tile : 128 * lane_tile + 128]

    pack_ends(read_residual, rf)
    for copy in ends(rf, xbuf, s_r, lambda g: r_rx.at[g]):
        copy.start()
    largest = jnp.max(jnp.abs(res[...]), axis=(0, 2))[:, None]
    power = jnp.floor(8.0 * jnp.log2(jnp.maximum(largest, 1e-30))) + 2.0
    power = jnp.broadcast_to(power, (ROWS, 128))
    to_unit = WHOLE * jnp.exp2(-0.125 * power)
    first_lane = iota((ROWS, 128), 1) == 0
    for index in range(TILES):
        piece = jnp.floor(window(read_residual, index) * to_unit + 0.5)
        rw[index] = jnp.where(first_lane, power, piece).astype(jnp.int32).astype(jnp.int16)
    to_windows(rw, rbuf, s_r, lambda g: r_r.at[g // BATCH], True)

    def send_error(level, core):
        own = (level == tm) & (core == 0)
        slot = jnp.where(own, TILES, tile)
        to_core = jnp.where(own, 1, core)
        return remote(
            ebuf.at[level, core], ebox.at[slot], s_e.at[level, core], r_e.at[slot], (level, to_core, sy)
        )

    right_tile = lax.rem(tile + 1, TILES)
    left_tile = lax.rem(tile + TILES - 1, TILES)
    right_sy = jnp.where(tile == TILES - 1, east, sy)
    left_sy = jnp.where(tile == 0, west, sy)
    refresh = [
        remote(mine, nbr.at[0], s_n.at[0], r_n.at[0], (owner_of(right_tile), 0, right_sy)),
        remote(mine, nbr.at[1], s_n.at[1], r_n.at[1], (owner_of(left_tile), 0, left_sy)),
    ]

    window_lane = iota((2 * ROWS, 128), 1)
    grid_row = iota((2 * ROWS, 128), 0)
    place = lax.rem(window_lane, 64)
    first = window_lane < 64
    from_extra = ((place < REACH) & (tile == 0)) | ((place >= 64 - REACH) & (tile == TILES - 1))
    outside = ((place < REACH) & (tile == 0) & (sy == 0)) | (
        (place >= 64 - REACH) & (tile == TILES - 1) & (sy == 3)
    )
    valid = (place[0 : ROWS // 2] >= REACH) & (place[0 : ROWS // 2] < 64 - REACH)
    keep = jnp.where(outside, 0.0, 1.0).astype(F32)
    top_open = jnp.where(grid_row == 2 * ROWS - 1, 0.0, 1.0).astype(F32)
    bottom_open = jnp.where(grid_row == 0, 0.0, 1.0).astype(F32)

    def unfold(part):
        pieces = [part[EDGE * core : EDGE * (core + 1)] for core in range(2)]
        step = jnp.where(tile == 0, 128 - REACH, REACH)
        return jnp.concatenate(
            [pltpu.roll(piece, lax.rem(step * i, 128), 1) for piece in pieces for i in range(ROWS // EDGE)], 0
        )

    @pl.when(is_owner)
    def _():
        def merge(level, _):
            arrived(vxbuf.at[level], r_vx.at[level])
            both = jnp.where(from_extra, unfold(vxbuf[level]), vbuf[level].astype(F32))
            vbuf[level] = both.astype(jnp.bfloat16)
            return 0

        def coarse_coefficients(level, _):
            v = vbuf[level].astype(F32) * keep
            after = jnp.where(level + 1 < GROUPS, c_ref[jnp.minimum(level + 1, GROUPS - 1)], 0)
            span = jnp.full((1, 128), STEPS + after - c_ref[level], jnp.int32).astype(F32)
            inverse = keep * (1.0 / (1.0 + 2.0 * span))
            k = span * inverse
            swapped = roll(v, 64, 1)
            u = jnp.where(first, v, swapped)
            w = jnp.where(first, swapped, v)
            dx = 0.5 * (roll(v, -1, 0) * top_open - roll(v, 1, 0) * bottom_open)
            dy = 0.5 * (roll(v, -1, 1) - roll(v, 1, 1))
            coef[level, 0] = inverse - k * jnp.where(first, dx, dy)
            coef[level, 1] = -k * jnp.where(first, roll(dx, 64, 1), roll(dy, 64, 1))
            coef[level, 2] = k * (0.5 + 0.5 * u) * top_open
            coef[level, 3] = k * (0.5 - 0.5 * u) * bottom_open
            coef[level, 4] = k * (0.5 + 0.5 * w)
            coef[level, 5] = k * (0.5 - 0.5 * w)
            return 0

        def prepare(low, high):
            arrived(vbuf.at[low:high], r_v.at[low // LEVELS])

            @pl.when(is_end)
            def _():
                lax.fori_loop(low, high, merge, 0)

            lax.fori_loop(low, high, coarse_coefficients, 0)

        prepare(GROUPS - LEVELS, GROUPS)
        prepare(0, GROUPS - LEVELS)

        def decode(last_level):
            arrived(rbuf.at[pl.ds(last_level, BATCH)], r_r.at[last_level // BATCH])
            for n in range(BATCH):
                level = last_level + n
                whole = rbuf[level].astype(jnp.int32).astype(F32)
                unit = jnp.exp2(0.125 * jnp.broadcast_to(whole[:, 0:1], whole.shape)) * (1.0 / WHOLE)
                dec[level] = whole * unit * keep

            @pl.when(is_end)
            def _():
                for n in range(BATCH):
                    level = last_level + n
                    arrived(xbuf.at[level], r_rx.at[level])
                    dec[level] = jnp.where(from_extra, unfold(xbuf[level]) * keep, dec[level])

        def solve(top, arriving):
            def several(turn, error):
                first_level = top - BATCH * turn
                if arriving:
                    decode(first_level - BATCH + 1)
                for n in range(BATCH):
                    level = first_level - n
                    c = [coef[level, i] for i in range(6)]
                    new = c[0] * error + c[1] * roll(error, 64, 1)
                    new = new + (c[2] * roll(error, -1, 0) + c[3] * roll(error, 1, 0))
                    new = new + (c[4] * roll(error, -1, 1) + c[5] * roll(error, 1, 1))
                    error = new + dec[level]
                    for core in range(2):
                        low = new[ROWS * core : ROWS * core + ROWS // 2]
                        high = new[ROWS * core + ROWS // 2 : ROWS * (core + 1)]
                        piece = jnp.where(valid, low, roll(high, 32, 1))
                        ebuf[level, core] = piece
                        if core == 0:
                            ebox[tile] = jnp.where(level == tm, piece, ebox[tile])
                        send_error(level, core).start()
                return error

            return several

        error = lax.fori_loop(0, LEVELS // BATCH, solve(GROUPS - 1, True), jnp.zeros((2 * ROWS, 128), F32))
        mine[...] = error
        for copy in refresh:
            copy.start()

        def decode_rest(turn, _):
            decode(BATCH * turn)
            return 0

        lax.fori_loop(0, (GROUPS - LEVELS) // BATCH, decode_rest, 0)
        for copy in refresh:
            copy.wait_recv()
        error = jnp.where(place < REACH, roll(nbr[0], -32, 1), error)
        error = jnp.where(place >= 64 - REACH, roll(nbr[1], 32, 1), error) * keep
        lax.fori_loop(0, LEVELS // BATCH, solve(GROUPS - LEVELS - 1, False), error)

    for copy in relays:
        copy.wait_send()
    for copy in (*ends(vf, vxbuf, s_v, lambda g: r_vx.at[g]), *ends(rf, xbuf, s_r, lambda g: r_rx.at[g])):
        copy.wait_send()
    to_windows(vw, vbuf, s_v, lambda g: r_v.at[g // LEVELS], False)
    to_windows(rw, rbuf, s_r, lambda g: r_r.at[g // BATCH], False)
    owner_chip = lax.rem(x, 2) == lax.rem(z, 2)

    @pl.when((sx == 1) & owner_chip)
    def _():
        unused_windows(vbuf, lambda g: r_v.at[g // LEVELS])
        unused_windows(rbuf, lambda g: r_r.at[g // BATCH])

    lane = iota((ROWS // 2, 128), 1)
    for lane_tile in (0, 3, 1, 2):
        lanes = slice(128 * lane_tile, 128 * lane_tile + 128)
        for index in range(4 * lane_tile, 4 * lane_tile + 4):
            pl.when(jnp.logical_not(is_owner & (index == tile)))(
                functools.partial(arrived, ebox.at[index], r_e.at[index])
            )
        for part in range(2):
            rows = slice(part * ROWS // 2, (part + 1) * ROWS // 2)
            for k in range(2):
                whole = None
                for i in range(4):
                    piece = roll(ebox[4 * lane_tile + i], 32 * i - REACH - 64 * k - 32 * part, 1)
                    whole = piece if whole is None else jnp.where(lane >= 32 * i, piece, whole)
                whole = upd[k, rows, lanes] + whole
                for j in range(STEPS):
                    out[j, k, rows, lanes] = jnp.where(here == j, whole, out[j, k, rows, lanes])

    @pl.when((sx == 1) & owner_chip)
    def _():
        arrived(ebox.at[TILES], r_e.at[TILES])

    @pl.when(is_owner)
    def _():
        for copy in refresh:
            copy.wait_send()

        def wait_errors(level, _):
            for core in range(2):
                send_error(level, core).wait_send()
            return 0

        lax.fori_loop(0, GROUPS, wait_errors, 0)


def shards(adjoint_guess, sources, velocities, c_points):
    dma = pltpu.SemaphoreType.DMA
    vmem = pl.BlockSpec(memory_space=pltpu.VMEM)
    return pl.pallas_call(
        kernel,
        out_shape=pltpu.VMEM(adjoint_guess.shape, F32),
        in_specs=[pl.BlockSpec(memory_space=pltpu.HBM)] * 4,
        out_specs=vmem,
        scratch_shapes=[
            pltpu.SMEM((GROUPS,), jnp.int32),
            pltpu.VMEM((STEPS, 2, ROWS, COLS), F32),
            pltpu.VMEM((STEPS, 2, ROWS, COLS), jnp.bfloat16),
            pltpu.VMEM((STEPS, 2, XROWS, XCOLS), F32),
            pltpu.VMEM((STEPS, 2, XROWS, XCOLS), F32),
            pltpu.VMEM((2, 2, XROWS, XCOLS), F32),
            pltpu.VMEM((2, 2, XROWS, XCOLS), F32),
            pltpu.VMEM((STEPS, 8, XROWS, XCOLS), F32),
            pltpu.VMEM((2, 3, ROWS, 128), F32),
            pltpu.VMEM((2, 3, XROWS, 128), F32),
            pltpu.VMEM((2, ROWS, 128), F32),
            pltpu.VMEM((2, EDGE, 128), F32),
            pltpu.VMEM((2, ROWS, COLS), jnp.int16),
            pltpu.VMEM((2, ROWS, COLS), jnp.int16),
            pltpu.VMEM((EDGE, 128), F32),
            pltpu.VMEM((EDGE, 128), F32),
            pltpu.VMEM((2, EDGE, 128), F32),
            pltpu.VMEM((2, EDGE, 128), F32),
            pltpu.VMEM((2, ROWS, COLS), F32),
            pltpu.VMEM((2, ROWS, COLS), F32),
            pltpu.VMEM((TILES, ROWS, 128), jnp.int16),
            pltpu.VMEM((2, EDGE, 128), F32),
            pltpu.VMEM((TILES, ROWS, 128), jnp.bfloat16),
            pltpu.VMEM((2, EDGE, 128), F32),
            pltpu.VMEM((GROUPS + 1, 2 * ROWS, 128), jnp.int16),
            pltpu.VMEM((GROUPS, 2 * EDGE, 128), F32),
            pltpu.VMEM((GROUPS + 1, 2 * ROWS, 128), jnp.bfloat16),
            pltpu.VMEM((GROUPS, 2 * EDGE, 128), F32),
            pltpu.VMEM((GROUPS, 6, 2 * ROWS, 128), F32),
            pltpu.VMEM((GROUPS, 2 * ROWS, 128), F32),
            pltpu.VMEM((GROUPS, 2, ROWS // 2, 128), F32),
            pltpu.VMEM((TILES + 1, ROWS // 2, 128), F32),
            pltpu.VMEM((2 * ROWS, 128), F32),
            pltpu.VMEM((2, 2 * ROWS, 128), F32),
            dma((7,)), dma((7,)), dma((7,)), dma((7,)),
            dma((TILES + 2,)), dma((GROUPS // LEVELS + 1,)), dma((GROUPS,)),
            dma((TILES + 2,)), dma((GROUPS // BATCH + 1,)), dma((GROUPS,)),
            dma((GROUPS, 2)), dma((TILES + 1,)), dma((2,)), dma((2,)), dma((4,)), pltpu.SemaphoreType.REGULAR,
        ],
        compiler_params=pltpu.CompilerParams(has_side_effects=True, collective_id=0, vmem_limit_bytes=58 * 1024 * 1024),
    )(c_points, adjoint_guess, sources, velocities)


def solution(mesh):
    placed = (P("tm", None, "sx", "sy"), P("tm", None, "sx", "sy"), P("tm", None, "sx", "sy"), P())
    return jax.shard_map(
        shards, mesh=mesh, in_specs=placed, out_specs=P("tm", None, "sx", "sy"), check_vma=False
    )
```
